256 devices in a mesh: depth: 8 (over x_hi, y), res: 32 (over z, x_lo, core).
Axes of the slice: x: 4 (x_hi: 2, x_lo: 2; x = x_hi * 2 + x_lo), y: 4, z: 8, core: 2. Of those that a mesh axis runs over, the one named last changes fastest.
Arguments:
- alignment_left: bfloat16 [2048, 32768], P('depth', 'res'), may hold values from -6 to 6
- alignment_right: bfloat16 [2048, 32768], P('depth', 'res'), may hold values from -6 to 6
- window_starts: int32 [8], replicated, may hold values from 0 to 1016
- outer_product_weight: bfloat16 [1024, 128], replicated, may hold values from -6 to 6
- outer_product_bias: float32 [128], replicated, may hold values from -3 to 3
- query_key_value_gate_weight: bfloat16 [128, 512], replicated, may hold values from -0.5 to 0.5
- output_weight: bfloat16 [128, 128], replicated, may hold values from -2 to 2
- triangle_pair_bias: bfloat16 [4, 1024, 1024], P(None, 'res'), may hold values from -3 to 260
- residue_chain: int32 [1024], replicated, may hold values from 0 to 7, never falling along the last dimension, each value on 1 to 256 neighbouring positions
- interchain_offset: float32 [4], replicated, may hold values from -3 to -0.5
Outputs:
- pair_strip: bfloat16 [64, 1024, 128], P('depth', 'res')
- update: bfloat16 [64, 1024, 128], P('depth', 'res')
The draws below stay inside these ranges and needn't reach their ends.
All inputs are finite; a program needn't handle non-finite values.
Results may differ from the reference program's by a relative error of at most 0.014.
Values may be sent and summed in bfloat16 or wider, within the bound.
A program may use at most 128 MiB of HBM per device.

```python
import math
import jax
import jax.numpy as jnp
import numpy as np
from jax import lax

PROJ_CHANNELS = 32
CZ = 128
H = 4
DH = 32
R_DEV = 8
SEQUENCE_COUNT = 2048
RESIDUE_COUNT = 1024
GROUPS = 8
R = 64


def draw_triangle_pair_bias(key, part):
    base_key = jax.random.fold_in(key, 11)
    row_key = jax.random.fold_in(key, 12)
    level_key = jax.random.fold_in(key, 13)
    first_key = jax.random.fold_in(key, 14)
    second_key = jax.random.fold_in(key, 15)
    forced_key = jax.random.fold_in(key, 16)
    background = jnp.clip(jax.random.normal(base_key, (H, RESIDUE_COUNT, RESIDUE_COUNT), jnp.float32), -3.0, 3.0)
    forced_row = jax.random.randint(forced_key, (), 0, RESIDUE_COUNT)
    forced = (jnp.arange(H)[:, None] == 0) & (jnp.arange(RESIDUE_COUNT)[None, :] == forced_row)
    chosen = (jax.random.randint(row_key, (H, RESIDUE_COUNT), 0, 64) == 0) | forced
    levels = jnp.array([110.0, 180.0, 260.0], jnp.float32)
    level_row = levels[jax.random.randint(level_key, (H, RESIDUE_COUNT), 0, 3)]
    level_row = jnp.where(forced, 260.0, level_row)
    first_col = jax.random.randint(first_key, (H, RESIDUE_COUNT), 0, RESIDUE_COUNT)
    second = (first_col + jax.random.randint(second_key, (H, RESIDUE_COUNT), 1, RESIDUE_COUNT)) % RESIDUE_COUNT
    column = jnp.arange(RESIDUE_COUNT)[None, None, :]
    peaked = jnp.where(column == first_col[:, :, None], level_row[:, :, None], jnp.where(column == second[:, :, None], level_row[:, :, None] - 2.0, background))
    return jnp.where(chosen[:, :, None], peaked, background).astype(jnp.bfloat16)


def set_ends(entries, rng, smallest, top_value):
    spot = [jax.random.randint(jax.random.fold_in(rng, axis), (), 0, length) for axis, length in enumerate(entries.shape)]
    widest = entries.shape.index(max(entries.shape))
    next_to = spot[:widest] + [(spot[widest] + 1) % entries.shape[widest]] + spot[widest + 1:]
    return entries.at[tuple(spot)].set(smallest).at[tuple(next_to)].set(top_value)


def level_of(key, dims, pieces, least, largest):
    def one(axis_at, shards_of):
        draws = jax.random.uniform(jax.random.fold_in(jax.random.fold_in(key, 6), axis_at), (shards_of,), jnp.float32, least / len(pieces), largest / len(pieces))
        return jnp.repeat(jnp.exp(draws), dims[axis_at] // shards_of).reshape((-1,) + (1,) * (len(dims) - axis_at - 1))

    factor_of = one(*pieces[0])
    for cut in pieces[1:]:
        factor_of = factor_of * one(*cut)
    return factor_of


def split_up(amount, total, most, skew):
    weights = [(1 << 20) // math.isqrt(grade ** skew) + 1 for grade in range(2, amount + 1)]
    spare, given = total - most - (amount - 1), [1] * (amount - 1)
    while spare > 0:
        movable = [i for i in range(amount - 1) if given[i] < most]
        pool, remaining = sum([weights[i] for i in movable]), spare
        for i in movable:
            extra = min(most - given[i], max(1, remaining * weights[i] // pool), spare)
            given[i] = given[i] + extra
            spare = spare - extra
    return np.array([most] + given)


def uneven(rng, amount, total, bound, lean):
    if amount == 2:
        one = jax.random.randint(rng, (), max(1, total - bound), min(bound, total - 1) + 1)
        return jnp.stack([one, total - one])
    sizes = jnp.asarray(split_up(amount, total, bound, lean), jnp.int32)
    couples = (amount - 1) // 2
    giver, taker = sizes[1:1 + 2 * couples:2], sizes[2:2 + 2 * couples:2]
    room = jnp.minimum(giver - 1, bound - taker)
    moved = jax.random.randint(jax.random.fold_in(rng, 1), (couples,), 0, 1 << 20) % (room + 1)
    sizes = sizes.at[1:1 + 2 * couples:2].set(giver - moved).at[2:2 + 2 * couples:2].set(taker + moved)
    return sizes[jax.random.permutation(jax.random.fold_in(rng, 2), amount)]


def noise(key, extent, spread, reach, shards=(), kind=jnp.bfloat16):
    values = jax.random.normal(key, extent, jnp.float32) * spread
    if len(shards) > 0:
        values = level_of(key, extent, shards, -0.22, 0.18) * values
    return jnp.clip(values, min=-reach, max=reach).astype(kind)


def setup_inputs(seed: int = 0) -> dict:
    seeds = jax.random.split(jax.random.key(seed), 11)
    alignment_left = noise(seeds[0], (SEQUENCE_COUNT, RESIDUE_COUNT * PROJ_CHANNELS), 1.0, 6.0, ((0, 8), (1, 32)))
    alignment_right = noise(seeds[1], (SEQUENCE_COUNT, RESIDUE_COUNT * PROJ_CHANNELS), 1.0, 6.0, ((0, 8), (1, 32)))
    window_starts = set_ends(jax.random.randint(seeds[2], (GROUPS,), 0, RESIDUE_COUNT - R_DEV + 1), jax.random.fold_in(seeds[2], 1), 0, RESIDUE_COUNT - R_DEV).astype(jnp.int32)
    outer_product_weight = noise(seeds[3], (PROJ_CHANNELS * PROJ_CHANNELS, CZ), (0.03 * SEQUENCE_COUNT ** 0.5), 6.0)
    outer_product_bias = noise(seeds[4], (CZ,), 0.5, 3.0, (), jnp.float32)
    query_key_value_gate_weight = noise(seeds[5], (CZ, 4 * CZ), CZ ** -0.5, 0.5)
    output_weight = noise(seeds[6], (CZ, CZ), (CZ // 16) ** -0.5, 2.0)
    triangle_pair_bias = draw_triangle_pair_bias(jax.random.fold_in(seeds[10], 71), 0)
    residue_chain = jnp.searchsorted(jnp.cumsum(uneven(seeds[8], 8, RESIDUE_COUNT, RESIDUE_COUNT // 4, 1)), jnp.arange(RESIDUE_COUNT), side="right").astype(jnp.int32)
    interchain_offset = jnp.clip(jax.random.uniform(seeds[9], (H,), jnp.float32, -3.0, -0.5), -3.0, -0.5)
    return dict(alignment_left=alignment_left, alignment_right=alignment_right, window_starts=window_starts, outer_product_weight=outer_product_weight, outer_product_bias=outer_product_bias, query_key_value_gate_weight=query_key_value_gate_weight, output_weight=output_weight, triangle_pair_bias=triangle_pair_bias, residue_chain=residue_chain, interchain_offset=interchain_offset)


epsilon = 1e-05

def layer_norm(values):
    average = lax.optimization_barrier(jnp.mean(values, axis=-1, keepdims=True))
    centred = values - average
    variance = lax.optimization_barrier(jnp.mean(centred * centred, axis=-1, keepdims=True))
    return centred * lax.rsqrt(variance + epsilon)

def reference(alignment_left, alignment_right, window_starts, outer_product_weight, outer_product_bias, query_key_value_gate_weight, output_weight, triangle_pair_bias, residue_chain, interchain_offset):
    gathered_left = alignment_left.reshape(SEQUENCE_COUNT, RESIDUE_COUNT, PROJ_CHANNELS)
    gathered_right = alignment_right.reshape(SEQUENCE_COUNT, RESIDUE_COUNT, PROJ_CHANNELS).astype(jnp.float32)
    row_ids = (window_starts[:, None] + jnp.arange(R_DEV, dtype=jnp.int32)[None, :]).astype(jnp.int32)
    weight = outer_product_weight.astype(jnp.float32)

    def outer_block(block_rows):
        picked = jnp.take(gathered_left, block_rows, axis=1).astype(jnp.float32)
        outer_prod = jnp.einsum('hbv,hqz->bqvz', picked, gathered_right, precision=lax.Precision.HIGHEST)
        flat_outer = outer_prod.reshape(R_DEV * RESIDUE_COUNT, PROJ_CHANNELS * PROJ_CHANNELS)
        projected = jnp.dot(flat_outer, weight, precision=lax.Precision.HIGHEST)
        return (projected / SEQUENCE_COUNT + outer_product_bias[None, :]).astype(jnp.bfloat16).reshape(R_DEV, RESIDUE_COUNT, CZ)
    pair_strip = lax.map(outer_block, row_ids).reshape(R, RESIDUE_COUNT, CZ)
    differ = (residue_chain[:, None] != residue_chain[None, :]).astype(jnp.float32)
    full_bias = triangle_pair_bias.astype(jnp.float32) + interchain_offset[:, None, None] * differ[None, :, :]
    score_scale = DH ** (-0.5)

    def attend_row(pair_row):
        normed = layer_norm(pair_row.astype(jnp.float32)).astype(jnp.bfloat16)
        projection = jnp.dot(normed, query_key_value_gate_weight, preferred_element_type=jnp.float32).astype(jnp.bfloat16)
        queries = projection[:, :CZ].reshape(RESIDUE_COUNT, H, DH).astype(jnp.float32)
        key_heads = projection[:, CZ:2 * CZ].reshape(RESIDUE_COUNT, H, DH).astype(jnp.float32)
        value_heads = projection[:, 2 * CZ:3 * CZ].reshape(RESIDUE_COUNT, H, DH).astype(jnp.float32)
        gate_pre = projection[:, 3 * CZ:].astype(jnp.float32)
        scores = jnp.einsum('qhd,khd->hqk', queries, key_heads, precision=lax.Precision.HIGHEST) * score_scale + full_bias
        row_max = lax.optimization_barrier(jnp.max(scores, axis=-1, keepdims=True))
        weights = jnp.exp(scores - row_max)
        denom = lax.optimization_barrier(jnp.sum(weights, axis=-1))
        rounded = lax.optimization_barrier(weights.astype(jnp.bfloat16)).astype(jnp.float32)
        attended = jnp.einsum('hqk,khd->qhd', rounded, value_heads, precision=lax.Precision.HIGHEST)
        attended = attended / jnp.transpose(denom)[:, :, None]
        gated_out = (jax.nn.sigmoid(gate_pre) * attended.reshape(RESIDUE_COUNT, CZ)).astype(jnp.bfloat16)
        return jnp.dot(gated_out, output_weight, preferred_element_type=jnp.float32).astype(jnp.bfloat16)
    update = lax.map(attend_row, pair_strip)
    return (pair_strip, update)
```

```python
import functools

import jax
import jax.numpy as jnp
from jax import lax
from jax.experimental import pallas as pl
from jax.experimental.pallas import tpu as pltpu
from jax.sharding import PartitionSpec as P

CH = 32
CZ = 128
H = 4
DH = 32
U = 8
EPS = 1e-05
MESH = pl.DeviceIdType.MESH
f32 = jnp.float32
bf16 = jnp.bfloat16


def dot(a, b):
    return jnp.dot(a, b, preferred_element_type=f32)


def dot_t(a, b):
    return lax.dot_general(a, b, (((1,), (1,)), ((), ())), preferred_element_type=f32)


def kernel(
    nd,
    nr,
    seqs,
    ws_ref,
    off_ref,
    left_ref,
    right_ref,
    w_ref,
    ob_ref,
    wqkvg_ref,
    wout_ref,
    tb_ref,
    chain_ref,
    pair_ref,
    upd_ref,
    l1,
    l1_tiles,
    sel_own,
    sel_in,
    band,
    r_t,
    r_p,
    w_f,
    wbd,
    bias_f,
    xs,
    part,
    rs_in,
    nb,
    qp,
    s0_s,
    s0_r,
    sx_s,
    sx_r,
    bz_s,
    bz_r,
    bx_s,
    bx_r,
    bc_s,
    bc_r,
    rs_s,
    rs_r,
    nz_s,
    nz_r,
    nx_s,
    nx_r,
    nc_s,
    nc_r,
):
    nz = nr // 4
    nm = nr // 2
    chunk = seqs // nm
    tok = left_ref.shape[1] // CH
    groups = nd
    gh = groups // 2
    half = gh * U * CH
    tiles_dev = left_ref.shape[1] // 128
    keys = nr * tok

    d = lax.axis_index("depth")
    r = lax.axis_index("res")
    z = r // 4
    x = (r // 2) % 2
    c = r % 2
    m = r // 2
    x_peer = z * 4 + (1 - x) * 2 + c
    c_peer = z * 4 + x * 2 + (1 - c)

    def remote(src, dst, send, recv, depth, res):
        return pltpu.make_async_remote_copy(
            src_ref=src,
            dst_ref=dst,
            send_sem=send,
            recv_sem=recv,
            device_id=(depth, res),
            device_id_type=MESH,
        )

    barrier = pltpu.get_barrier_semaphore()

    @pl.loop(1, nm)
    def _(k):
        other = lax.rem(m + k, nm)
        pl.semaphore_signal(barrier, inc=1, device_id=(d, other * 2 + c), device_id_type=MESH)

    @pl.loop(1, nd)
    def _(k):
        pl.semaphore_signal(barrier, inc=1, device_id=(lax.rem(d + k, nd), r), device_id_type=MESH)

    pl.semaphore_signal(barrier, inc=1, device_id=(d, c_peer), device_id_type=MESH)
    pl.semaphore_wait(barrier, nm - 1 + nd - 1 + 1)

    def scatter_copy(k):
        other = lax.rem(m + k, nm)
        return remote(
            left_ref.at[pl.ds(other * chunk, chunk), :],
            l1.at[m],
            s0_s.at[k],
            s0_r.at[k],
            d,
            other * 2 + c,
        )

    @pl.loop(1, nm)
    def _(k):
        scatter_copy(k).start()

    l1[m] = left_ref[pl.ds(pl.multiple_of(m * chunk, chunk), chunk), :]

    for q in range(seqs // 128):
        r_t[q] = jnp.transpose(right_ref[q * 128 : (q + 1) * 128, :].astype(f32))
    w_f[...] = w_ref[...].astype(f32)
    wbd[...] = jnp.zeros_like(wbd)
    for i in range(CH):
        for q in range(seqs // 128):
            r_p[i * tok : (i + 1) * tok, q * 128 : (q + 1) * 128] = r_t[
                q, pl.ds(i, tok, stride=CH), :
            ].astype(bf16)
        w_i = w_f[pl.ds(i, CH, stride=CH), :].astype(bf16)
        for b in range(4):
            wbd[i * 128 + b * CH : i * 128 + (b + 1) * CH, b * CZ : (b + 1) * CZ] = w_i

    chain = chain_ref[...]
    key_at = lax.broadcasted_iota(jnp.int32, (tok, keys), 1)
    query_at = lax.broadcasted_iota(jnp.int32, (tok, keys), 0) + r * tok
    own = jnp.sum(jnp.where(key_at == query_at, chain, 0).astype(f32), axis=1, keepdims=True)
    differ = (own != chain.astype(f32)).astype(f32)
    for h in range(H):
        bias_f[h * tok : (h + 1) * tok, :] = tb_ref[h].astype(f32) + off_ref[h] * differ

    @pl.loop(1, nm)
    def _(k):
        scatter_copy(k).wait()

    for i in range(nm):
        for t in range(tiles_dev):
            l1_tiles[i * tiles_dev + t] = l1[i, :, t * 128 : (t + 1) * 128]

    last_tile = nr * tiles_dev - 1
    for g in range(groups):
        start = ws_ref[g]
        first = lax.div(start, 4)
        shift = start - 4 * first
        pieces = []
        for t in range(3):
            tile = jnp.minimum(first + t, last_tile)
            src = lax.div(tile, tiles_dev)
            chip = lax.div(src, 2)
            piece = l1_tiles[chip * tiles_dev + tile - src * tiles_dev].astype(f32)
            pieces.append(jnp.where(src - 2 * chip == c, piece, 0.0))
        wide = jnp.concatenate(pieces, axis=1)
        picked = wide[:, :256]
        for b in range(1, 4):
            picked = jnp.where(shift == b, wide[:, b * CH : b * CH + 256], picked)
        sel_own[g // gh, :, (g % gh) * 256 : (g % gh + 1) * 256] = picked.astype(bf16)

    swap = remote(sel_own.at[1 - c], sel_in, sx_s, sx_r, d, c_peer)
    swap.start()
    swap.wait()
    band[c, pl.ds(pl.multiple_of(m * chunk, chunk), chunk), :] = (
        sel_own[c].astype(f32) + sel_in[...].astype(f32)
    ).astype(bf16)

    def gather(block, z_s, z_r, x_s, x_r, c_s, c_r):
        def to_z(k):
            zz = lax.rem(z + k, nz)
            ref = block(r)
            return remote(ref, ref, z_s.at[k], z_r.at[k], d, zz * 4 + x * 2 + c)

        def to_x(k):
            ref = block(lax.rem(z + nz - k, nz) * 4 + x * 2 + c)
            return remote(ref, ref, x_s.at[k], x_r.at[k], d, x_peer)

        def to_c(k):
            zz = lax.rem(z + nz - lax.rem(k, nz), nz)
            xx = lax.rem(x + k // nz, 2)
            ref = block(zz * 4 + xx * 2 + c)
            return remote(ref, ref, c_s.at[k], c_r.at[k], d, c_peer)

        def begin():
            @pl.loop(1, nz)
            def _(k):
                to_z(k).start()

            to_x(0).start()
            to_c(0).start()

        def finish_own():
            @pl.loop(1, nz)
            def _(i):
                k = lax.rem(i, 2) * ((i + 1) // 2) + (1 - lax.rem(i, 2)) * (nz - i // 2)
                to_z(k).wait_recv()
                to_x(k).start()
                to_c(k).start()

            @pl.loop(0, nz)
            def _(k):
                to_x(k).wait_recv()
                to_c(nz + k).start()

        def finish_other():
            @pl.loop(0, 2 * nz)
            def _(k):
                to_c(k).wait_recv()

        def drain():
            @pl.loop(1, nz)
            def _(k):
                to_z(k).wait_send()

            @pl.loop(0, nz)
            def _(k):
                to_x(k).wait_send()

            @pl.loop(0, 2 * nz)
            def _(k):
                to_c(k).wait_send()

        return begin, finish_own, finish_other, drain

    begin, finish_own, finish_other, drain_band = gather(
        lambda res: band.at[res % 2, pl.ds((res // 2) * chunk, chunk), :],
        bz_s,
        bz_r,
        bx_s,
        bx_r,
        bc_s,
        bc_r,
    )
    begin()
    finish_own()

    def reduce_copy(g):
        return remote(part.at[g], rs_in.at[d], rs_s.at[g], rs_r.at[d], g, r)

    def outer(side):
        for i in range(gh):
            y = dot(r_p[...], band[side, :, i * 256 : (i + 1) * 256]).astype(bf16)
            for t in range(2):
                for e in range(CH):
                    row = (2 * i + t) * tok
                    xs[row : row + tok, e * 128 : (e + 1) * 128] = y[
                        e * tok : (e + 1) * tok, t * 128 : (t + 1) * 128
                    ]
        out = dot(xs[...], wbd[...]).astype(bf16)
        for i in range(gh):
            g = side * gh + i
            for u in range(U):
                row = (2 * i + u // 4) * tok
                part[g, u * tok : (u + 1) * tok, :] = out[
                    row : row + tok, (u % 4) * CZ : (u % 4 + 1) * CZ
                ]

            @pl.when(g != d)
            def _():
                reduce_copy(g).start()

    outer(c)
    finish_other()
    outer(1 - c)
    rs_in[d] = part[d]

    @pl.loop(1, nd)
    def _(k):
        src = lax.rem(d + k, nd)
        remote(part.at[src], rs_in.at[src], rs_s.at[src], rs_r.at[src], src, r).wait()

    total = rs_in[0].astype(f32)
    for k in range(1, nd):
        total = total + rs_in[k].astype(f32)
    pair = (total * (1.0 / (seqs * nd)) + ob_ref[...]).astype(bf16)
    pair_ref[...] = pair.reshape(U, tok, CZ)
    value = pair.astype(f32)
    centred = value - jnp.mean(value, axis=1, keepdims=True)
    variance = jnp.mean(centred * centred, axis=1, keepdims=True)
    normed = (centred * lax.rsqrt(variance + EPS)).astype(bf16)
    nb[:, pl.ds(pl.multiple_of(r * tok, tok), tok), :] = normed.reshape(U, tok, CZ)

    begin, finish_own, finish_other, drain_normed = gather(
        lambda res: nb.at[:, pl.ds(res * tok, tok), :],
        nz_s,
        nz_r,
        nx_s,
        nx_r,
        nc_s,
        nc_r,
    )
    begin()
    queries = dot(normed, wqkvg_ref[:, :CZ]).astype(bf16)
    gate = jax.nn.sigmoid(dot(normed, wqkvg_ref[:, 3 * CZ :]).astype(bf16).astype(f32))
    head_of = lax.broadcasted_iota(jnp.int32, (U * tok, CZ), 1) // DH
    for h in range(H):
        own_head = jnp.where(head_of == h, queries, jnp.zeros_like(queries))
        key_side = (dot_t(own_head, wqkvg_ref[:, CZ : 2 * CZ]) * (DH**-0.5)).astype(bf16)
        for u in range(U):
            qp[u, h * tok : (h + 1) * tok, :] = key_side[u * tok : (u + 1) * tok, :]
    finish_own()
    finish_other()

    head_lane = lax.broadcasted_iota(jnp.int32, (tok, CZ), 1) // DH
    for u in range(U):
        rows = nb[u]
        scores = dot_t(qp[u], rows) + bias_f[...]
        top = jnp.max(scores, axis=1, keepdims=True)
        weights = jnp.exp(scores - top)
        denom = jnp.sum(weights, axis=1, keepdims=True)
        mixed = dot(weights.astype(bf16), rows) / denom
        values = dot(mixed.astype(bf16), wqkvg_ref[:, 2 * CZ : 3 * CZ])
        attended = jnp.zeros((tok, CZ), f32)
        for h in range(H):
            attended = jnp.where(head_lane == h, values[h * tok : (h + 1) * tok, :], attended)
        gated = (gate[u * tok : (u + 1) * tok, :] * attended).astype(bf16)
        upd_ref[u] = dot(gated, wout_ref[...]).astype(bf16)

    drain_band()
    drain_normed()


def body(
    nd,
    nr,
    alignment_left,
    alignment_right,
    window_starts,
    outer_product_weight,
    outer_product_bias,
    query_key_value_gate_weight,
    output_weight,
    triangle_pair_bias,
    residue_chain,
    interchain_offset,
):
    seqs, cols = alignment_left.shape
    tok = cols // CH
    nz, nm = nr // 4, nr // 2
    chunk = seqs // nm
    half = (nd // 2) * U * CH
    keys = nr * tok
    vmem = pl.BlockSpec(memory_space=pltpu.VMEM)
    smem = pl.BlockSpec(memory_space=pltpu.SMEM)
    sem = pltpu.SemaphoreType.DMA
    out = jax.ShapeDtypeStruct((U, tok, CZ), bf16)
    return pl.pallas_call(
        functools.partial(kernel, nd, nr, seqs),
        out_shape=(out, out),
        in_specs=[smem, smem] + [vmem] * 8,
        out_specs=(vmem, vmem),
        scratch_shapes=[
            pltpu.VMEM((nm, chunk, cols), bf16),
            pltpu.VMEM((nm * cols // 128, chunk, 128), bf16),
            pltpu.VMEM((2, chunk, half), bf16),
            pltpu.VMEM((chunk, half), bf16),
            pltpu.VMEM((2, seqs, half), bf16),
            pltpu.VMEM((seqs // 128, cols, 128), f32),
            pltpu.VMEM((cols, seqs), bf16),
            pltpu.VMEM((CH * CH, CZ), f32),
            pltpu.VMEM((CH * 128, 4 * CZ), bf16),
            pltpu.VMEM((H * tok, keys), f32),
            pltpu.VMEM((nd // 2 * 2 * tok, CH * 128), bf16),
            pltpu.VMEM((nd, U * tok, CZ), bf16),
            pltpu.VMEM((nd, U * tok, CZ), bf16),
            pltpu.VMEM((U, keys, CZ), bf16),
            pltpu.VMEM((U, H * tok, CZ), bf16),
            sem((nm,)),
            sem((nm,)),
            sem,
            sem,
            sem((nz,)),
            sem((nz,)),
            sem((nz,)),
            sem((nz,)),
            sem((2 * nz,)),
            sem((2 * nz,)),
            sem((nd,)),
            sem((nd,)),
            sem((nz,)),
            sem((nz,)),
            sem((nz,)),
            sem((nz,)),
            sem((2 * nz,)),
            sem((2 * nz,)),
        ],
        compiler_params=pltpu.CompilerParams(
            collective_id=0, has_side_effects=True, vmem_limit_bytes=50 * 1024 * 1024
        ),
        cost_estimate=pl.CostEstimate(
            flops=4_000_000_000, bytes_accessed=4_000_000, transcendentals=1_100_000
        ),
    )(
        window_starts,
        interchain_offset,
        alignment_left,
        alignment_right,
        outer_product_weight,
        outer_product_bias.reshape(1, CZ),
        query_key_value_gate_weight,
        output_weight,
        triangle_pair_bias,
        residue_chain.reshape(1, keys),
    )


def solution(mesh):
    in_specs = (
        P("depth", "res"),
        P("depth", "res"),
        P(),
        P(),
        P(),
        P(),
        P(),
        P(None, "res", None),
        P(),
        P(),
    )
    out_specs = (P("depth", "res", None), P("depth", "res", None))
    return jax.shard_map(
        functools.partial(body, mesh.shape["depth"], mesh.shape["res"]),
        mesh=mesh,
        in_specs=in_specs,
        out_specs=out_specs,
        check_vma=False,
    )
```

```python
import functools

import jax
import jax.numpy as jnp
from jax import lax
from jax.experimental import pallas as pl
from jax.experimental.pallas import tpu as pltpu
from jax.sharding import PartitionSpec as P

CH = 32
CZ = 128
H = 4
DH = 32
U = 8
EPS = 1e-05
VMEM_BYTES = 63 * 1024 * 1024
MESH = pl.DeviceIdType.MESH
f32 = jnp.float32
bf16 = jnp.bfloat16


def dot(a, b):
    return jnp.dot(a, b, preferred_element_type=f32)


def dot_t(a, b):
    return lax.dot_general(a, b, (((1,), (1,)), ((), ())), preferred_element_type=f32)


def kernel(
    nd,
    nr,
    ws_ref,
    off_ref,
    left_hbm,
    right_hbm,
    w_hbm,
    ob_hbm,
    wqkvg_hbm,
    wout_hbm,
    tb_hbm,
    chain_hbm,
    pair_ref,
    upd_ref,
    right,
    w,
    ob,
    wqkvg,
    wout,
    chain_v,
    tb,
    l1,
    l1_tiles,
    picks,
    picks_in,
    band,
    r_t,
    r_p,
    w_f,
    wbd,
    bias_f,
    xs,
    part,
    rs_in,
    rows_out,
    nb,
    ub,
    upd_in,
    in_sem,
    s0_s,
    s0_r,
    tb_s,
    tb_r,
    pk_s,
    pk_r,
    bz_s,
    bz_r,
    bx_s,
    bx_r,
    bc_s,
    bc_r,
    rs_s,
    rs_r,
    ex_s,
    ex_r,
    nz_s,
    nz_r,
    up_s,
    up_r,
):
    seqs, cols = left_hbm.shape
    tok = cols // CH
    nz = nr // 4
    hops = nz // 2
    chunk = seqs // nz
    groups = nd
    quarter = groups // 4 * U * CH
    gq = groups // 4
    tiles_dev = cols // 128
    keys = nr * tok
    level = 4 * tok

    d = lax.axis_index("depth")
    r = lax.axis_index("res")
    z = r // 4
    p = r % 4
    x = p // 2
    c = p % 2
    p_x = (1 - x) * 2 + c
    p_c = x * 2 + (1 - c)
    p_xc = (1 - x) * 2 + (1 - c)

    def remote(src, dst, send, recv, depth, res):
        return pltpu.make_async_remote_copy(
            src_ref=src,
            dst_ref=dst,
            send_sem=send,
            recv_sem=recv,
            device_id=(depth, res),
            device_id_type=MESH,
        )

    barrier = pltpu.get_barrier_semaphore()
    others = (p_x, p_c, p_xc)
    for k in range(1, nz):
        pl.semaphore_signal(
            barrier, inc=1, device_id=(d, lax.rem(z + k, nz) * 4 + p), device_id_type=MESH
        )
    for q in others:
        pl.semaphore_signal(barrier, inc=1, device_id=(d, z * 4 + q), device_id_type=MESH)
    for k in range(1, nd):
        pl.semaphore_signal(barrier, inc=1, device_id=(lax.rem(d + k, nd), r), device_id_type=MESH)

    inputs = [
        pltpu.make_async_copy(src, dst, in_sem.at[i])
        for i, (src, dst) in enumerate(
            (
                (right_hbm, right),
                (w_hbm, w),
                (ob_hbm, ob),
                (wqkvg_hbm, wqkvg),
                (wout_hbm, wout),
                (chain_hbm, chain_v),
                (tb_hbm, tb.at[p]),
                (left_hbm.at[pl.ds(z * chunk, chunk), :], l1.at[z]),
            )
        )
    ]
    for copy in inputs:
        copy.start()
    pl.semaphore_wait(barrier, nz - 1 + 3 + nd - 1)

    def scatter_copy(k):
        zz = lax.rem(z + k, nz)
        return remote(
            left_hbm.at[pl.ds(zz * chunk, chunk), :],
            l1.at[z],
            s0_s.at[k],
            s0_r.at[k],
            d,
            zz * 4 + p,
        )

    order = sorted(range(1, nz), key=lambda k: -min(k, nz - k))
    for k in order:
        scatter_copy(k).start()

    for copy in inputs:
        copy.wait()
    tb_own_x = remote(tb.at[p], tb.at[p], tb_s.at[0], tb_r.at[0], d, z * 4 + p_x)
    tb_own_c = remote(tb.at[p], tb.at[p], tb_s.at[1], tb_r.at[1], d, z * 4 + p_c)
    tb_x_c = remote(tb.at[p_x], tb.at[p_x], tb_s.at[2], tb_r.at[2], d, z * 4 + p_c)
    tb_own_x.start()
    tb_own_c.start()

    for q in range(seqs // 128):
        r_t[q] = jnp.transpose(right[q * 128 : (q + 1) * 128, :].astype(f32))
    w_f[...] = w[...].astype(f32)
    wbd[...] = jnp.zeros_like(wbd)
    for i in range(CH):
        for q in range(seqs // 128):
            r_p[i * tok : (i + 1) * tok, q * 128 : (q + 1) * 128] = r_t[
                q, pl.ds(i, tok, stride=CH), :
            ].astype(bf16)
        w_i = w_f[pl.ds(i, CH, stride=CH), :].astype(bf16)
        for b in range(4):
            wbd[i * 128 + b * CH : i * 128 + (b + 1) * CH, b * CZ : (b + 1) * CZ] = w_i

    for k in order:
        scatter_copy(k).wait()

    for i in range(nz):
        for t in range(tiles_dev):
            l1_tiles[i * tiles_dev + t] = l1[i, :, t * 128 : (t + 1) * 128]

    last_tile = nr * tiles_dev - 1
    for g in range(groups):
        start = ws_ref[g]
        first = lax.div(start, 4)
        shift = start - 4 * first
        pieces = []
        for t in range(3):
            tile = jnp.minimum(first + t, last_tile)
            src = lax.div(tile, tiles_dev)
            zz = lax.div(src, 4)
            piece = l1_tiles[zz * tiles_dev + tile - src * tiles_dev].astype(f32)
            pieces.append(jnp.where(src - 4 * zz == p, piece, 0.0))
        wide = jnp.concatenate(pieces, axis=1)
        picked = wide[:, :256]
        for b in range(1, 4):
            picked = jnp.where(shift == b, wide[:, b * CH : b * CH + 256], picked)
        picks[g // gq, :, (g % gq) * 256 : (g % gq + 1) * 256] = picked.astype(bf16)

    picks_out = [
        remote(picks.at[q], picks_in.at[p], pk_s.at[q], pk_r.at[p], d, z * 4 + q) for q in others
    ]
    for copy in picks_out:
        copy.start()
    tb_own_x.wait_recv()
    tb_x_c.start()
    for q, copy in zip(others, picks_out):
        copy.wait_send()
        remote(picks.at[q], picks_in.at[q], pk_s.at[q], pk_r.at[q], d, z * 4 + q).wait_recv()
    picks_in[p] = picks[p]
    merged = picks_in[0].astype(f32)
    for q in range(1, 4):
        merged = merged + picks_in[q].astype(f32)
    band[p, pl.ds(pl.multiple_of(z * chunk, chunk), chunk), :] = merged.astype(bf16)

    def ring(block, halves, send, recv, arrived):
        def hop(s, left):
            at = lax.rem(z + (s - 1 if left else nz + 1 - s), nz)
            nxt = lax.rem(z + (nz - 1 if left else 1), nz)
            ref = halves(at, int(left)) if s == hops else block(at)
            i = (s - 1) * 2 + int(left)
            return remote(ref, ref, send.at[i], recv.at[i], d, nxt * 4 + p)

        hop(1, False).start()
        hop(1, True).start()
        arrived(0)
        for s in range(1, hops):
            hop(s, False).wait_recv()
            hop(s + 1, False).start()
            hop(s, True).wait_recv()
            hop(s + 1, True).start()
            arrived(s)
            arrived(nz - s)
        hop(hops, False).wait_recv()
        hop(hops, True).wait_recv()
        arrived(hops)

        def drain():
            for s in range(1, hops + 1):
                hop(s, False).wait_send()
                hop(s, True).wait_send()

        return drain

    def band_x(k, sender):
        zz = lax.rem(z + nz - k, nz)
        ref = band.at[p if sender else p_x, pl.ds(zz * chunk, chunk), :]
        return remote(ref, ref, bx_s.at[k], bx_r.at[k], d, z * 4 + p_x)

    drain_band = ring(
        lambda zz: band.at[p, pl.ds(zz * chunk, chunk), :],
        lambda zz, i: band.at[p, pl.ds(zz * chunk + i * (chunk // 2), chunk // 2), :],
        bz_s,
        bz_r,
        lambda k: band_x(k, True).start(),
    )

    def band_c(i, q):
        return remote(band.at[q], band.at[q], bc_s.at[i], bc_r.at[i], d, z * 4 + p_c)

    band_c(0, p).start()

    def reduce_copy(g):
        return remote(part.at[g], rs_in.at[d], rs_s.at[g], rs_r.at[d], g, r)

    def spread(side, q):
        for i in range(gq):
            y = dot(r_p[...], band[q, :, i * 256 : (i + 1) * 256]).astype(bf16)
            for t in range(2):
                row = (side * 2 * gq + 2 * i + t) * tok
                for e in range(CH):
                    xs[row : row + tok, e * 128 : (e + 1) * 128] = y[
                        e * tok : (e + 1) * tok, t * 128 : (t + 1) * 128
                    ]

    def project(pair_of_quarters):
        out = dot(xs[...], wbd[...]).astype(bf16)
        for side, q in enumerate(pair_of_quarters):
            for i in range(gq):
                g = q * gq + i
                for u in range(U):
                    row = (side * 2 * gq + 2 * i + u // 4) * tok
                    part[g, u * tok : (u + 1) * tok, :] = out[
                        row : row + tok, (u % 4) * CZ : (u % 4 + 1) * CZ
                    ]

                @pl.when(g != d)
                def _():
                    reduce_copy(g).start()

    spread(0, p)
    band_c(0, p_c).wait_recv()
    spread(1, p_c)
    for k in range(nz):
        band_x(k, False).wait_recv()
    band_c(1, p_x).start()
    project((p, p_c))
    spread(0, p_x)
    band_c(1, p_xc).wait_recv()
    spread(1, p_xc)
    project((p_x, p_xc))
    rs_in[d] = part[d]

    tb_own_c.wait_recv()
    tb_x_c.wait_recv()
    chain = chain_v[...]
    key_at = lax.broadcasted_iota(jnp.int32, (level, keys), 1)
    query_at = lax.broadcasted_iota(jnp.int32, (level, keys), 0) + z * level
    chain_f = chain.astype(f32)
    own = jnp.sum(jnp.where(key_at == query_at, chain_f, 0.0), axis=1, keepdims=True)
    differ = (own != chain_f).astype(f32)
    for h in range(H):
        for q in range(4):
            row = h * level + q * tok
            bias_f[row : row + tok, :] = (
                tb[q, h].astype(f32) + off_ref[h] * differ[q * tok : (q + 1) * tok, :]
            )

    for k in range(1, nd):
        src = lax.rem(d + k, nd)
        remote(part.at[src], rs_in.at[src], rs_s.at[src], rs_r.at[src], src, r).wait()

    total = rs_in[0].astype(f32)
    for k in range(1, nd):
        total = total + rs_in[k].astype(f32)
    pair = (total * (1.0 / (seqs * nd)) + ob[...]).astype(bf16)
    pair_ref[...] = pair.reshape(U, tok, CZ)
    value = pair.astype(f32)
    centred = value - jnp.mean(value, axis=1, keepdims=True)
    variance = jnp.mean(centred * centred, axis=1, keepdims=True)
    rows_out[...] = (centred * lax.rsqrt(variance + EPS)).astype(bf16).reshape(U, tok, CZ)

    mine = pl.ds(pl.multiple_of(r * tok, tok), tok)

    def rows_copy(q, src_p):
        at = pl.ds((z * 4 + src_p) * tok, tok)
        return remote(
            rows_out.at[pl.ds(q * 2, 2)], nb.at[:, at, :], ex_s.at[q], ex_r.at[src_p], d, z * 4 + q
        )

    for q in others:
        rows_copy(q, p).start()
    for i in range(2):
        nb[i, mine, :] = rows_out[2 * p + i]
    for q in others:
        rows_copy(q, q).wait_recv()

    drain_rows = ring(
        lambda zz: nb.at[:, pl.ds(zz * level, level), :],
        lambda zz, i: nb.at[i, pl.ds(zz * level, level), :],
        nz_s,
        nz_r,
        lambda k: None,
    )

    head_lane = lax.broadcasted_iota(jnp.int32, (level, CZ), 1) // DH
    for i in range(2):
        rows = nb[i]
        near = nb[i, pl.ds(pl.multiple_of(z * level, level), level), :]
        queries = dot(near, wqkvg[:, :CZ]).astype(bf16)
        gate = jax.nn.sigmoid(dot(near, wqkvg[:, 3 * CZ :]).astype(bf16).astype(f32))
        attended = jnp.zeros((level, CZ), f32)
        for h in range(H):
            own_head = jnp.where(head_lane == h, queries, jnp.zeros_like(queries))
            key_side = (dot_t(own_head, wqkvg[:, CZ : 2 * CZ]) * (DH**-0.5)).astype(bf16)
            scores = dot_t(key_side, rows) + bias_f[h * level : (h + 1) * level, :]
            top = jnp.max(scores, axis=1, keepdims=True)
            weights = jnp.exp(scores - top)
            denom = jnp.sum(weights, axis=1, keepdims=True)
            mixed = dot(weights.astype(bf16), rows) / denom
            values = dot(mixed.astype(bf16), wqkvg[:, 2 * CZ : 3 * CZ])
            attended = jnp.where(head_lane == h, values, attended)
        gated = (gate * attended).astype(bf16)
        ub[i] = dot(gated, wout[...]).astype(bf16)

    def upd_copy(q, src_p):
        return remote(
            ub.at[:, pl.ds(q * tok, tok), :],
            upd_in.at[src_p],
            up_s.at[q],
            up_r.at[src_p],
            d,
            z * 4 + q,
        )

    for q in others:
        upd_copy(q, p).start()
    upd_in[p] = ub[:, pl.ds(pl.multiple_of(p * tok, tok), tok), :]
    for q in others:
        upd_copy(q, q).wait_recv()
    for q in range(4):
        for i in range(2):
            upd_ref[2 * q + i] = upd_in[q, i]

    tb_own_x.wait_send()
    tb_own_c.wait_send()
    tb_x_c.wait_send()
    drain_band()
    for k in range(nz):
        band_x(k, True).wait_send()
    band_c(0, p).wait_send()
    band_c(1, p_x).wait_send()
    drain_rows()
    for q in others:
        rows_copy(q, p).wait_send()
        upd_copy(q, p).wait_send()


def body(
    nd,
    nr,
    alignment_left,
    alignment_right,
    window_starts,
    outer_product_weight,
    outer_product_bias,
    query_key_value_gate_weight,
    output_weight,
    triangle_pair_bias,
    residue_chain,
    interchain_offset,
):
    seqs, cols = alignment_left.shape
    tok = cols // CH
    nz = nr // 4
    chunk = seqs // nz
    quarter = nd // 4 * U * CH
    keys = nr * tok
    anywhere = pl.BlockSpec(memory_space=pl.ANY)
    vmem = pl.BlockSpec(memory_space=pltpu.VMEM)
    smem = pl.BlockSpec(memory_space=pltpu.SMEM)
    sem = pltpu.SemaphoreType.DMA
    out = jax.ShapeDtypeStruct((U, tok, CZ), bf16)
    return pl.pallas_call(
        functools.partial(kernel, nd, nr),
        out_shape=(out, out),
        in_specs=[smem, smem] + [anywhere] * 8,
        out_specs=(vmem, vmem),
        scratch_shapes=[
            pltpu.VMEM((seqs, cols), bf16),
            pltpu.VMEM((CH * CH, CZ), bf16),
            pltpu.VMEM((1, CZ), f32),
            pltpu.VMEM((CZ, 4 * CZ), bf16),
            pltpu.VMEM((CZ, CZ), bf16),
            pltpu.VMEM((1, keys), jnp.int32),
            pltpu.VMEM((4, H, tok, keys), bf16),
            pltpu.VMEM((nz, chunk, cols), bf16),
            pltpu.VMEM((nz * cols // 128, chunk, 128), bf16),
            pltpu.VMEM((4, chunk, quarter), bf16),
            pltpu.VMEM((4, chunk, quarter), bf16),
            pltpu.VMEM((4, seqs, quarter), bf16),
            pltpu.VMEM((seqs // 128, cols, 128), f32),
            pltpu.VMEM((cols, seqs), bf16),
            pltpu.VMEM((CH * CH, CZ), f32),
            pltpu.VMEM((CH * 128, 4 * CZ), bf16),
            pltpu.VMEM((H * 4 * tok, keys), f32),
            pltpu.VMEM((nd // 2 * 2 * tok, CH * 128), bf16),
            pltpu.VMEM((nd, U * tok, CZ), bf16),
            pltpu.VMEM((nd, U * tok, CZ), bf16),
            pltpu.VMEM((U, tok, CZ), bf16),
            pltpu.VMEM((2, keys, CZ), bf16),
            pltpu.VMEM((2, 4 * tok, CZ), bf16),
            pltpu.VMEM((4, 2, tok, CZ), bf16),
            sem((8,)),
            sem((nz,)),
            sem((nz,)),
            sem((3,)),
            sem((3,)),
            sem((4,)),
            sem((4,)),
            sem((nz,)),
            sem((nz,)),
            sem((nz,)),
            sem((nz,)),
            sem((2,)),
            sem((2,)),
            sem((nd,)),
            sem((nd,)),
            sem((4,)),
            sem((4,)),
            sem((nz,)),
            sem((nz,)),
            sem((4,)),
            sem((4,)),
        ],
        compiler_params=pltpu.CompilerParams(
            collective_id=0, has_side_effects=True, vmem_limit_bytes=VMEM_BYTES
        ),
        cost_estimate=pl.CostEstimate(
            flops=4_000_000_000, bytes_accessed=4_000_000, transcendentals=1_100_000
        ),
    )(
        window_starts,
        interchain_offset,
        alignment_left,
        alignment_right,
        outer_product_weight,
        outer_product_bias.reshape(1, CZ),
        query_key_value_gate_weight,
        output_weight,
        triangle_pair_bias,
        residue_chain.reshape(1, keys),
    )


def solution(mesh):
    in_specs = (
        P("depth", "res"),
        P("depth", "res"),
        P(),
        P(),
        P(),
        P(),
        P(),
        P(None, "res", None),
        P(),
        P(),
    )
    out_specs = (P("depth", "res", None), P("depth", "res", None))
    return jax.shard_map(
        functools.partial(body, mesh.shape["depth"], mesh.shape["res"]),
        mesh=mesh,
        in_specs=in_specs,
        out_specs=out_specs,
        check_vma=False,
    )
```

```python
import functools

import jax
import jax.numpy as jnp
from jax import lax
from jax.experimental import pallas as pl
from jax.experimental.pallas import tpu as pltpu
from jax.sharding import PartitionSpec as P

CH = 32
CZ = 128
H = 4
DH = 32
U = 8
EPS = 1e-05
VMEM_BYTES = 63 * 1024 * 1024
MESH = pl.DeviceIdType.MESH
f32 = jnp.float32
bf16 = jnp.bfloat16


def dot(a, b):
    return jnp.dot(a, b, preferred_element_type=f32)


def dot_t(a, b):
    return lax.dot_general(a, b, (((1,), (1,)), ((), ())), preferred_element_type=f32)


def kernel(
    nd,
    nr,
    ws_ref,
    off_ref,
    left_hbm,
    right_hbm,
    w_hbm,
    ob_hbm,
    wqkvg_hbm,
    wout_hbm,
    tb_hbm,
    chain_hbm,
    pair_ref,
    upd_ref,
    right,
    w,
    ob,
    wqkvg,
    wout,
    chain_v,
    tb,
    l1,
    l1_tiles,
    picks,
    picks_in,
    band,
    r_t,
    r_p,
    w_f,
    wbd,
    bias_f,
    xs,
    part,
    rs_in,
    rows_out,
    nb,
    qp,
    ub,
    upd_in,
    in_sem,
    s0_s,
    s0_r,
    tb_s,
    tb_r,
    pk_s,
    pk_r,
    bz_s,
    bz_r,
    bx_s,
    bx_r,
    bc_s,
    bc_r,
    rs_s,
    rs_r,
    ex_s,
    ex_r,
    nz_s,
    nz_r,
    up_s,
    up_r,
):
    seqs, cols = left_hbm.shape
    tok = cols // CH
    nz = nr // 4
    chunk = seqs // nz
    groups = nd
    quarter = groups // 4 * U * CH
    gq = groups // 4
    tiles_dev = cols // 128
    keys = nr * tok
    level = 4 * tok

    d = lax.axis_index("depth")
    r = lax.axis_index("res")
    z = r // 4
    p = r % 4
    x = p // 2
    c = p % 2
    p_x = (1 - x) * 2 + c
    p_c = x * 2 + (1 - c)
    p_xc = (1 - x) * 2 + (1 - c)

    def remote(src, dst, send, recv, depth, res):
        return pltpu.make_async_remote_copy(
            src_ref=src,
            dst_ref=dst,
            send_sem=send,
            recv_sem=recv,
            device_id=(depth, res),
            device_id_type=MESH,
        )

    barrier = pltpu.get_barrier_semaphore()
    others = (p_x, p_c, p_xc)
    for k in range(1, nz):
        pl.semaphore_signal(
            barrier, inc=1, device_id=(d, lax.rem(z + k, nz) * 4 + p), device_id_type=MESH
        )
    for q in others:
        pl.semaphore_signal(barrier, inc=1, device_id=(d, z * 4 + q), device_id_type=MESH)
    for k in range(1, nd):
        pl.semaphore_signal(barrier, inc=1, device_id=(lax.rem(d + k, nd), r), device_id_type=MESH)

    inputs = [
        pltpu.make_async_copy(src, dst, in_sem.at[i])
        for i, (src, dst) in enumerate(
            (
                (right_hbm, right),
                (w_hbm, w),
                (ob_hbm, ob),
                (wqkvg_hbm, wqkvg),
                (wout_hbm, wout),
                (chain_hbm, chain_v),
                (tb_hbm, tb.at[p]),
                (left_hbm.at[pl.ds(z * chunk, chunk), :], l1.at[z]),
            )
        )
    ]
    for copy in inputs:
        copy.start()
    pl.semaphore_wait(barrier, nz - 1 + 3 + nd - 1)

    def scatter_copy(k):
        zz = lax.rem(z + k, nz)
        return remote(
            left_hbm.at[pl.ds(zz * chunk, chunk), :],
            l1.at[z],
            s0_s.at[k],
            s0_r.at[k],
            d,
            zz * 4 + p,
        )

    order = sorted(range(1, nz), key=lambda k: -min(k, nz - k))
    for k in order:
        scatter_copy(k).start()

    for copy in inputs:
        copy.wait()
    tb_own_x = remote(tb.at[p], tb.at[p], tb_s.at[0], tb_r.at[0], d, z * 4 + p_x)
    tb_own_c = remote(tb.at[p], tb.at[p], tb_s.at[1], tb_r.at[1], d, z * 4 + p_c)
    tb_x_c = remote(tb.at[p_x], tb.at[p_x], tb_s.at[2], tb_r.at[2], d, z * 4 + p_c)
    tb_own_x.start()
    tb_own_c.start()

    for q in range(seqs // 128):
        r_t[q] = jnp.transpose(right[q * 128 : (q + 1) * 128, :].astype(f32))
    w_f[...] = w[...].astype(f32)
    wbd[...] = jnp.zeros_like(wbd)
    for i in range(CH):
        for q in range(seqs // 128):
            r_p[i * tok : (i + 1) * tok, q * 128 : (q + 1) * 128] = r_t[
                q, pl.ds(i, tok, stride=CH), :
            ].astype(bf16)
        w_i = w_f[pl.ds(i, CH, stride=CH), :].astype(bf16)
        for b in range(4):
            wbd[i * 128 + b * CH : i * 128 + (b + 1) * CH, b * CZ : (b + 1) * CZ] = w_i

    for k in order:
        scatter_copy(k).wait()

    for i in range(nz):
        for t in range(tiles_dev):
            l1_tiles[i * tiles_dev + t] = l1[i, :, t * 128 : (t + 1) * 128]

    last_tile = nr * tiles_dev - 1
    for g in range(groups):
        start = ws_ref[g]
        first = lax.div(start, 4)
        shift = start - 4 * first
        pieces = []
        for t in range(3):
            tile = jnp.minimum(first + t, last_tile)
            src = lax.div(tile, tiles_dev)
            zz = lax.div(src, 4)
            piece = l1_tiles[zz * tiles_dev + tile - src * tiles_dev].astype(f32)
            pieces.append(jnp.where(src - 4 * zz == p, piece, 0.0))
        wide = jnp.concatenate(pieces, axis=1)
        picked = wide[:, :256]
        for b in range(1, 4):
            picked = jnp.where(shift == b, wide[:, b * CH : b * CH + 256], picked)
        picks[g // gq, :, (g % gq) * 256 : (g % gq + 1) * 256] = picked.astype(bf16)

    picks_out = [
        remote(picks.at[q], picks_in.at[p], pk_s.at[q], pk_r.at[p], d, z * 4 + q) for q in others
    ]
    for copy in picks_out:
        copy.start()
    tb_own_x.wait_recv()
    tb_x_c.start()
    for q, copy in zip(others, picks_out):
        copy.wait_send()
        remote(picks.at[q], picks_in.at[q], pk_s.at[q], pk_r.at[q], d, z * 4 + q).wait_recv()
    picks_in[p] = picks[p]
    merged = picks_in[0].astype(f32)
    for q in range(1, 4):
        merged = merged + picks_in[q].astype(f32)
    band[p, pl.ds(pl.multiple_of(z * chunk, chunk), chunk), :] = merged.astype(bf16)

    near = sorted(range(1, nz), key=lambda k: min(k, nz - k))

    def gather(block, send, recv):
        def copy(k, back):
            zz = lax.rem(z + (nz - k if back else k), nz)
            ref = block(zz if back else z)
            return remote(ref, ref, send.at[k], recv.at[k], d, zz * 4 + p)

        for k in near:
            copy(k, False).start()

        def arrive(k):
            copy(k, True).wait_recv()

        def drain():
            for k in near:
                copy(k, False).wait_send()

        return arrive, drain

    def band_x(k, sender):
        zz = lax.rem(z + nz - k, nz)
        ref = band.at[p if sender else p_x, pl.ds(zz * chunk, chunk), :]
        return remote(ref, ref, bx_s.at[k], bx_r.at[k], d, z * 4 + p_x)

    band_arrive, drain_band = gather(
        lambda zz: band.at[p, pl.ds(zz * chunk, chunk), :], bz_s, bz_r
    )
    band_x(0, True).start()
    for k in near:
        band_arrive(k)
        band_x(k, True).start()

    def band_c(i, q):
        return remote(band.at[q], band.at[q], bc_s.at[i], bc_r.at[i], d, z * 4 + p_c)

    band_c(0, p).start()

    def reduce_copy(g):
        return remote(part.at[g], rs_in.at[d], rs_s.at[g], rs_r.at[d], g, r)

    def spread(side, q):
        for i in range(gq):
            y = dot(r_p[...], band[q, :, i * 256 : (i + 1) * 256]).astype(bf16)
            for t in range(2):
                row = (side * 2 * gq + 2 * i + t) * tok
                for e in range(CH):
                    xs[row : row + tok, e * 128 : (e + 1) * 128] = y[
                        e * tok : (e + 1) * tok, t * 128 : (t + 1) * 128
                    ]

    def project(pair_of_quarters):
        out = dot(xs[...], wbd[...]).astype(bf16)
        for side, q in enumerate(pair_of_quarters):
            for i in range(gq):
                g = q * gq + i
                for u in range(U):
                    row = (side * 2 * gq + 2 * i + u // 4) * tok
                    part[g, u * tok : (u + 1) * tok, :] = out[
                        row : row + tok, (u % 4) * CZ : (u % 4 + 1) * CZ
                    ]

                @pl.when(g != d)
                def _():
                    reduce_copy(g).start()

    spread(0, p)
    band_c(0, p_c).wait_recv()
    spread(1, p_c)
    for k in range(nz):
        band_x(k, False).wait_recv()
    band_c(1, p_x).start()
    project((p, p_c))
    spread(0, p_x)
    band_c(1, p_xc).wait_recv()
    spread(1, p_xc)
    project((p_x, p_xc))
    rs_in[d] = part[d]

    tb_own_c.wait_recv()
    tb_x_c.wait_recv()
    chain = chain_v[...]
    key_at = lax.broadcasted_iota(jnp.int32, (level, keys), 1)
    query_at = lax.broadcasted_iota(jnp.int32, (level, keys), 0) + z * level
    chain_f = chain.astype(f32)
    own = jnp.sum(jnp.where(key_at == query_at, chain_f, 0.0), axis=1, keepdims=True)
    differ = (own != chain_f).astype(f32)
    for h in range(H):
        for q in range(4):
            row = h * level + q * tok
            bias_f[row : row + tok, :] = (
                tb[q, h].astype(f32) + off_ref[h] * differ[q * tok : (q + 1) * tok, :]
            )

    for k in range(1, nd):
        src = lax.rem(d + k, nd)
        remote(part.at[src], rs_in.at[src], rs_s.at[src], rs_r.at[src], src, r).wait()

    total = rs_in[0].astype(f32)
    for k in range(1, nd):
        total = total + rs_in[k].astype(f32)
    pair = (total * (1.0 / (seqs * nd)) + ob[...]).astype(bf16)
    pair_ref[...] = pair.reshape(U, tok, CZ)
    value = pair.astype(f32)
    centred = value - jnp.mean(value, axis=1, keepdims=True)
    variance = jnp.mean(centred * centred, axis=1, keepdims=True)
    rows_out[...] = (centred * lax.rsqrt(variance + EPS)).astype(bf16).reshape(U, tok, CZ)

    mine = pl.ds(pl.multiple_of(r * tok, tok), tok)

    def rows_copy(q, src_p):
        at = pl.ds((z * 4 + src_p) * tok, tok)
        return remote(
            rows_out.at[pl.ds(q * 2, 2)], nb.at[:, at, :], ex_s.at[q], ex_r.at[src_p], d, z * 4 + q
        )

    for q in others:
        rows_copy(q, p).start()
    for i in range(2):
        nb[i, mine, :] = rows_out[2 * p + i]
    for q in others:
        rows_copy(q, q).wait_recv()

    rows_arrive, drain_rows = gather(
        lambda zz: nb.at[:, pl.ds(zz * level, level), :], nz_s, nz_r
    )

    head_lane = lax.broadcasted_iota(jnp.int32, (level, CZ), 1) // DH
    gates = []
    for i in range(2):
        here = nb[i, pl.ds(pl.multiple_of(z * level, level), level), :]
        queries = dot(here, wqkvg[:, :CZ]).astype(bf16)
        gates.append(jax.nn.sigmoid(dot(here, wqkvg[:, 3 * CZ :]).astype(bf16).astype(f32)))
        for h in range(H):
            own_head = jnp.where(head_lane == h, queries, jnp.zeros_like(queries))
            key_side = dot_t(own_head, wqkvg[:, CZ : 2 * CZ]) * (DH**-0.5)
            qp[i, h * level : (h + 1) * level, :] = key_side.astype(bf16)

    top, denom, mixed = [None, None], [None, None], [None, None]
    for ks in [(0,)] + [(k, nz - k) for k in range(1, nz // 2)] + [(nz // 2,)]:
        for k in ks:
            if k:
                rows_arrive(k)
        ats = [pl.ds(pl.multiple_of(lax.rem(z + nz - k, nz) * level, level), level) for k in ks]
        offsets = jnp.concatenate([bias_f[:, at] for at in ats], axis=1)
        for i in range(2):
            rows = jnp.concatenate([nb[i, at, :] for at in ats], axis=0)
            scores = dot_t(qp[i], rows) + offsets
            peak = jnp.max(scores, axis=1, keepdims=True)
            if ks == (0,):
                weights = jnp.exp(scores - peak)
                denom[i] = jnp.sum(weights, axis=1, keepdims=True)
                mixed[i] = dot(weights.astype(bf16), rows)
            else:
                peak = jnp.maximum(peak, top[i])
                shrink = jnp.exp(top[i] - peak)
                weights = jnp.exp(scores - peak)
                denom[i] = denom[i] * shrink + jnp.sum(weights, axis=1, keepdims=True)
                mixed[i] = mixed[i] * shrink + dot(weights.astype(bf16), rows)
            top[i] = peak

    for i in range(2):
        values = dot((mixed[i] / denom[i]).astype(bf16), wqkvg[:, 2 * CZ : 3 * CZ])
        attended = jnp.zeros((level, CZ), f32)
        for h in range(H):
            attended = jnp.where(head_lane == h, values[h * level : (h + 1) * level, :], attended)
        ub[i] = dot((gates[i] * attended).astype(bf16), wout[...]).astype(bf16)

    def upd_copy(q, src_p):
        return remote(
            ub.at[:, pl.ds(q * tok, tok), :],
            upd_in.at[src_p],
            up_s.at[q],
            up_r.at[src_p],
            d,
            z * 4 + q,
        )

    for q in others:
        upd_copy(q, p).start()
    upd_in[p] = ub[:, pl.ds(pl.multiple_of(p * tok, tok), tok), :]
    for q in others:
        upd_copy(q, q).wait_recv()
    for q in range(4):
        for i in range(2):
            upd_ref[2 * q + i] = upd_in[q, i]

    tb_own_x.wait_send()
    tb_own_c.wait_send()
    tb_x_c.wait_send()
    drain_band()
    for k in range(nz):
        band_x(k, True).wait_send()
    band_c(0, p).wait_send()
    band_c(1, p_x).wait_send()
    drain_rows()
    for q in others:
        rows_copy(q, p).wait_send()
        upd_copy(q, p).wait_send()


def body(
    nd,
    nr,
    alignment_left,
    alignment_right,
    window_starts,
    outer_product_weight,
    outer_product_bias,
    query_key_value_gate_weight,
    output_weight,
    triangle_pair_bias,
    residue_chain,
    interchain_offset,
):
    seqs, cols = alignment_left.shape
    tok = cols // CH
    nz = nr // 4
    chunk = seqs // nz
    quarter = nd // 4 * U * CH
    keys = nr * tok
    anywhere = pl.BlockSpec(memory_space=pl.ANY)
    vmem = pl.BlockSpec(memory_space=pltpu.VMEM)
    smem = pl.BlockSpec(memory_space=pltpu.SMEM)
    sem = pltpu.SemaphoreType.DMA
    out = jax.ShapeDtypeStruct((U, tok, CZ), bf16)
    return pl.pallas_call(
        functools.partial(kernel, nd, nr),
        out_shape=(out, out),
        in_specs=[smem, smem] + [anywhere] * 8,
        out_specs=(vmem, vmem),
        scratch_shapes=[
            pltpu.VMEM((seqs, cols), bf16),
            pltpu.VMEM((CH * CH, CZ), bf16),
            pltpu.VMEM((1, CZ), f32),
            pltpu.VMEM((CZ, 4 * CZ), bf16),
            pltpu.VMEM((CZ, CZ), bf16),
            pltpu.VMEM((1, keys), jnp.int32),
            pltpu.VMEM((4, H, tok, keys), bf16),
            pltpu.VMEM((nz, chunk, cols), bf16),
            pltpu.VMEM((nz * cols // 128, chunk, 128), bf16),
            pltpu.VMEM((4, chunk, quarter), bf16),
            pltpu.VMEM((4, chunk, quarter), bf16),
            pltpu.VMEM((4, seqs, quarter), bf16),
            pltpu.VMEM((seqs // 128, cols, 128), f32),
            pltpu.VMEM((cols, seqs), bf16),
            pltpu.VMEM((CH * CH, CZ), f32),
            pltpu.VMEM((CH * 128, 4 * CZ), bf16),
            pltpu.VMEM((H * 4 * tok, keys), f32),
            pltpu.VMEM((nd // 2 * 2 * tok, CH * 128), bf16),
            pltpu.VMEM((nd, U * tok, CZ), bf16),
            pltpu.VMEM((nd, U * tok, CZ), bf16),
            pltpu.VMEM((U, tok, CZ), bf16),
            pltpu.VMEM((2, keys, CZ), bf16),
            pltpu.VMEM((2, H * 4 * tok, CZ), bf16),
            pltpu.VMEM((2, 4 * tok, CZ), bf16),
            pltpu.VMEM((4, 2, tok, CZ), bf16),
            sem((8,)),
            sem((nz,)),
            sem((nz,)),
            sem((3,)),
            sem((3,)),
            sem((4,)),
            sem((4,)),
            sem((nz,)),
            sem((nz,)),
            sem((nz,)),
            sem((nz,)),
            sem((2,)),
            sem((2,)),
            sem((nd,)),
            sem((nd,)),
            sem((4,)),
            sem((4,)),
            sem((nz,)),
            sem((nz,)),
            sem((4,)),
            sem((4,)),
        ],
        compiler_params=pltpu.CompilerParams(
            collective_id=0, has_side_effects=True, vmem_limit_bytes=VMEM_BYTES
        ),
        cost_estimate=pl.CostEstimate(
            flops=4_000_000_000, bytes_accessed=4_000_000, transcendentals=1_100_000
        ),
    )(
        window_starts,
        interchain_offset,
        alignment_left,
        alignment_right,
        outer_product_weight,
        outer_product_bias.reshape(1, CZ),
        query_key_value_gate_weight,
        output_weight,
        triangle_pair_bias,
        residue_chain.reshape(1, keys),
    )


def solution(mesh):
    in_specs = (
        P("depth", "res"),
        P("depth", "res"),
        P(),
        P(),
        P(),
        P(),
        P(),
        P(None, "res", None),
        P(),
        P(),
    )
    out_specs = (P("depth", "res", None), P("depth", "res", None))
    return jax.shard_map(
        functools.partial(body, mesh.shape["depth"], mesh.shape["res"]),
        mesh=mesh,
        in_specs=in_specs,
        out_specs=out_specs,
        check_vma=False,
    )
```

```python
import functools

import jax
import jax.numpy as jnp
from jax import lax
from jax.experimental import pallas as pl
from jax.experimental.pallas import tpu as pltpu
from jax.sharding import PartitionSpec as P

CH = 32
CZ = 128
H = 4
DH = 32
U = 8
EPS = 1e-05
VMEM_BYTES = 63 * 1024 * 1024
MESH = pl.DeviceIdType.MESH
f32 = jnp.float32
bf16 = jnp.bfloat16


def dot(a, b):
    return jnp.dot(a, b, preferred_element_type=f32)


def dot_t(a, b):
    return lax.dot_general(a, b, (((1,), (1,)), ((), ())), preferred_element_type=f32)


def kernel(
    nd,
    nr,
    ws_ref,
    off_ref,
    left_hbm,
    right_hbm,
    w_hbm,
    ob_hbm,
    wqkvg_hbm,
    wout_hbm,
    tb_hbm,
    chain_hbm,
    pair_ref,
    upd_ref,
    right,
    w,
    ob,
    wqkvg,
    wout,
    chain_v,
    tb,
    l1,
    l1_tiles,
    picks,
    picks_in,
    band,
    r_t,
    r_p,
    w_f,
    wbd,
    bias_f,
    xs,
    part,
    rs_in,
    pair_out,
    pair_in,
    nb,
    qp,
    ub,
    upd_in,
    in_sem,
    s0_s,
    s0_r,
    tb_s,
    tb_r,
    pk_s,
    pk_r,
    bz_s,
    bz_r,
    rx_s,
    rx_r,
    bc_s,
    bc_r,
    rs_s,
    rs_r,
    pr_s,
    pr_r,
    nz_s,
    nz_r,
    up_s,
    up_r,
):
    seqs, cols = left_hbm.shape
    tok = cols // CH
    nz = nr // 4
    chunk = seqs // nz
    groups = nd
    gq = groups // 4
    gh = groups // 2
    tiles_dev = cols // 128
    keys = nr * tok
    level = 4 * tok

    d = lax.axis_index("depth")
    r = lax.axis_index("res")
    z = r // 4
    p = r % 4
    x = p // 2
    c = p % 2
    p_x = (1 - x) * 2 + c
    p_c = x * 2 + (1 - c)
    p_xc = (1 - x) * 2 + (1 - c)

    def remote(src, dst, send, recv, depth, res):
        return pltpu.make_async_remote_copy(
            src_ref=src,
            dst_ref=dst,
            send_sem=send,
            recv_sem=recv,
            device_id=(depth, res),
            device_id_type=MESH,
        )

    barrier = pltpu.get_barrier_semaphore()
    others = (p_x, p_c, p_xc)
    for k in range(1, nz):
        pl.semaphore_signal(
            barrier, inc=1, device_id=(d, lax.rem(z + k, nz) * 4 + p), device_id_type=MESH
        )
    for q in others:
        pl.semaphore_signal(barrier, inc=1, device_id=(d, z * 4 + q), device_id_type=MESH)
    for k in range(1, nd):
        for e in range(2):
            pl.semaphore_signal(
                barrier,
                inc=1,
                device_id=(lax.rem(d + k, nd), z * 4 + d // gh * 2 + e),
                device_id_type=MESH,
            )

    inputs = [
        pltpu.make_async_copy(src, dst, in_sem.at[i])
        for i, (src, dst) in enumerate(
            (
                (right_hbm, right.at[x]),
                (w_hbm, w),
                (ob_hbm, ob),
                (wqkvg_hbm, wqkvg),
                (wout_hbm, wout),
                (chain_hbm, chain_v),
                (tb_hbm, tb.at[p]),
                (left_hbm.at[pl.ds(z * chunk, chunk), :], l1.at[z]),
            )
        )
    ]
    for copy in inputs:
        copy.start()
    apart = (d // gh - x) * (d // gh - x)
    pl.semaphore_wait(barrier, nz - 1 + 3 + 4 * (gh - 1) + 4 * apart)

    def scatter_copy(k):
        zz = lax.rem(z + k, nz)
        return remote(
            left_hbm.at[pl.ds(zz * chunk, chunk), :],
            l1.at[z],
            s0_s.at[k],
            s0_r.at[k],
            d,
            zz * 4 + p,
        )

    order = sorted(range(1, nz), key=lambda k: -min(k, nz - k))
    for k in order:
        scatter_copy(k).start()

    right_copy = remote(right_hbm, right.at[x], rx_s.at[0], rx_r.at[0], d, z * 4 + p_x)
    right_copy.start()

    for copy in inputs:
        copy.wait()
    tb_own_x = remote(tb.at[p], tb.at[p], tb_s.at[0], tb_r.at[0], d, z * 4 + p_x)
    tb_own_c = remote(tb.at[p], tb.at[p], tb_s.at[1], tb_r.at[1], d, z * 4 + p_c)
    tb_x_c = remote(tb.at[p_x], tb.at[p_x], tb_s.at[2], tb_r.at[2], d, z * 4 + p_c)

    def turn_right(b):
        for q in range(seqs // 128):
            r_t[q] = jnp.transpose(right[b, q * 128 : (q + 1) * 128, :].astype(f32))
        for i in range(CH):
            row = pl.ds(pl.multiple_of((2 * i + b) * tok, tok), tok)
            for q in range(seqs // 128):
                r_p[row, q * 128 : (q + 1) * 128] = r_t[q, pl.ds(i, tok, stride=CH), :].astype(bf16)

    turn_right(x)
    w_f[...] = w[...].astype(f32)
    wbd[...] = jnp.zeros_like(wbd)
    for i in range(CH):
        w_i = w_f[pl.ds(i, CH, stride=CH), :].astype(bf16)
        for b in range(4):
            wbd[i * 128 + b * CH : i * 128 + (b + 1) * CH, b * CZ : (b + 1) * CZ] = w_i

    for k in order:
        scatter_copy(k).wait()

    for i in range(nz):
        for t in range(tiles_dev):
            l1_tiles[i * tiles_dev + t] = l1[i, :, t * 128 : (t + 1) * 128]

    last_tile = nr * tiles_dev - 1
    for g in range(groups):
        start = ws_ref[g]
        first = lax.div(start, 4)
        shift = start - 4 * first
        pieces = []
        for t in range(3):
            tile = jnp.minimum(first + t, last_tile)
            src = lax.div(tile, tiles_dev)
            zz = lax.div(src, 4)
            piece = l1_tiles[zz * tiles_dev + tile - src * tiles_dev].astype(f32)
            pieces.append(jnp.where(src - 4 * zz == p, piece, 0.0))
        wide = jnp.concatenate(pieces, axis=1)
        picked = wide[:, :256]
        for b in range(1, 4):
            picked = jnp.where(shift == b, wide[:, b * CH : b * CH + 256], picked)
        picks[g // gq, :, (g % gq) * 256 : (g % gq + 1) * 256] = picked.astype(bf16)

    picks_out = [
        remote(picks.at[q], picks_in.at[p], pk_s.at[q], pk_r.at[p], d, z * 4 + q) for q in others
    ]
    for copy in picks_out:
        copy.start()
    right_copy.wait()
    tb_own_x.start()
    tb_own_c.start()
    turn_right(1 - x)
    for q, copy in zip(others, picks_out):
        copy.wait_send()
        remote(picks.at[q], picks_in.at[q], pk_s.at[q], pk_r.at[q], d, z * 4 + q).wait_recv()
    picks_in[p] = picks[p]
    merged = picks_in[0].astype(f32)
    for q in range(1, 4):
        merged = merged + picks_in[q].astype(f32)
    band[c, pl.ds(pl.multiple_of(z * chunk, chunk), chunk), :] = merged.astype(bf16)

    near = sorted(range(1, nz), key=lambda k: min(k, nz - k))

    def gather(block, send, recv):
        def copy(k, back):
            zz = lax.rem(z + (nz - k if back else k), nz)
            ref = block(zz if back else z)
            return remote(ref, ref, send.at[k], recv.at[k], d, zz * 4 + p)

        for k in near:
            copy(k, False).start()

        def arrive(k):
            copy(k, True).wait_recv()

        def drain():
            for k in near:
                copy(k, False).wait_send()

        return arrive, drain

    band_arrive, drain_band = gather(
        lambda zz: band.at[c, pl.ds(zz * chunk, chunk), :], bz_s, bz_r
    )
    for k in near:
        band_arrive(k)

    def band_c(q):
        return remote(band.at[q], band.at[q], bc_s.at[0], bc_r.at[0], d, z * 4 + p_c)

    band_c(c).start()

    def reduce_copy(i, q, g, depth, e):
        return remote(
            part.at[i, q], rs_in.at[depth * 2 + e], rs_s.at[i * 4 + q], rs_r.at[depth * 2 + e], g, z * 4 + q
        )

    def outer(e):
        for i in range(gq):
            y = dot(r_p[...], band[e, :, i * 256 : (i + 1) * 256]).astype(bf16)
            for t in range(2):
                row = (2 * i + t) * 2 * tok
                for b in range(CH):
                    xs[row : row + 2 * tok, b * 128 : (b + 1) * 128] = y[
                        b * 2 * tok : (b + 1) * 2 * tok, t * 128 : (t + 1) * 128
                    ]
        out = dot(xs[...], wbd[...]).astype(bf16)
        for i in range(gq):
            at = e * gq + i
            g = x * gh + at
            for q in range(4):
                for n in range(2):
                    u = 2 * q + n
                    for b in range(2):
                        row = ((2 * i + u // 4) * 2 + b) * tok
                        part[at, q, n, b] = out[row : row + tok, (u % 4) * CZ : (u % 4 + 1) * CZ]

                here = jnp.logical_and(g == d, q == p)

                @pl.when(jnp.logical_not(here))
                def _():
                    reduce_copy(at, q, g, d, c).start()

                @pl.when(here)
                def _():
                    rs_in[d * 2 + c] = part[at, q]

    outer(c)
    band_c(1 - c).wait_recv()
    tb_own_x.wait_recv()
    tb_x_c.start()
    outer(1 - c)

    tb_own_c.wait_recv()
    tb_x_c.wait_recv()
    chain = chain_v[...]
    key_at = lax.broadcasted_iota(jnp.int32, (level, keys), 1)
    query_at = lax.broadcasted_iota(jnp.int32, (level, keys), 0) + z * level
    chain_f = chain.astype(f32)
    own = jnp.sum(jnp.where(key_at == query_at, chain_f, 0.0), axis=1, keepdims=True)
    differ = (own != chain_f).astype(f32)
    for h in range(H):
        for q in range(4):
            row = h * level + q * tok
            bias_f[row : row + tok, :] = (
                tb[q, h].astype(f32) + off_ref[h] * differ[q * tok : (q + 1) * tok, :]
            )

    def reduced(depth, e):
        return remote(
            part.at[0, 0],
            rs_in.at[depth * 2 + e],
            rs_s.at[0],
            rs_r.at[depth * 2 + e],
            depth,
            z * 4 + d // gh * 2 + e,
        )

    for e in range(2):
        for k in range(nd):
            source = lax.rem(d + k, nd)
            if k == 0:

                @pl.when(jnp.logical_not(jnp.logical_and(d // gh == x, c == e)))
                def _():
                    reduced(d, e).wait_recv()

            else:
                reduced(source, e).wait_recv()

        total = rs_in[e].astype(f32)
        for k in range(1, nd):
            total = total + rs_in[2 * k + e].astype(f32)
        total = total.reshape(4 * tok, CZ)
        pair = (total * (1.0 / (seqs * nd)) + ob[...]).astype(bf16)
        value = pair.astype(f32)
        centred = value - jnp.mean(value, axis=1, keepdims=True)
        variance = jnp.mean(centred * centred, axis=1, keepdims=True)
        normed = (centred * lax.rsqrt(variance + EPS)).astype(bf16)
        for n in range(2):
            for b in range(2):
                piece = slice((2 * n + b) * tok, (2 * n + b + 1) * tok)
                to = pl.ds(pl.multiple_of((z * 4 + 2 * b + e) * tok, tok), tok)
                nb[n, to, :] = normed[piece]
                pair_out[2 * b + e, n] = pair[piece]

    def rows_copy(k, to, at, i=None):
        rows = pl.ds(lax.rem(z + nz + at, nz) * level, level)
        ref = nb.at[:, rows, :] if i is None else nb.at[i, rows, :]
        return remote(ref, ref, nz_s.at[k], nz_r.at[k], d, lax.rem(z + nz + to, nz) * 4 + p)

    if nz == 8:
        first = [rows_copy(k, k, 0) for k in (2, 6, 1, 7)]
        onward = {
            2: [rows_copy(3, 1, -2), rows_copy(4, 2, -2, 0)],
            6: [rows_copy(5, -1, 2), rows_copy(0, -2, 2, 1)],
        }
        landing = {k: [rows_copy(k, 0, -k)] for k in (1, 2, 3, 5, 6, 7)}
        landing[4] = [rows_copy(4, 0, 4, 0), rows_copy(0, 0, 4, 1)]
        turns = [(0,), (2, 6), (1, 7), (3, 5), (4,)]
    else:
        first = [rows_copy(k, k, 0) for k in near]
        onward = {}
        landing = {k: [rows_copy(k, 0, -k)] for k in near}
        turns = [(0,)] + [(k, nz - k) for k in range(1, nz // 2)] + [(nz // 2,)]
    for copy in first:
        copy.start()

    def pair_copy(q, src_p):
        return remote(
            pair_out.at[q], pair_in.at[src_p], pr_s.at[q], pr_r.at[src_p], d, z * 4 + q
        )

    for q in others:
        pair_copy(q, p).start()
    pair_in[p] = pair_out[p]

    head_lane = lax.broadcasted_iota(jnp.int32, (level, CZ), 1) // DH
    gates = []
    for i in range(2):
        here = nb[i, pl.ds(pl.multiple_of(z * level, level), level), :]
        queries = dot(here, wqkvg[:, :CZ]).astype(bf16)
        gates.append(jax.nn.sigmoid(dot(here, wqkvg[:, 3 * CZ :]).astype(bf16).astype(f32)))
        for h in range(H):
            own_head = jnp.where(head_lane == h, queries, jnp.zeros_like(queries))
            key_side = dot_t(own_head, wqkvg[:, CZ : 2 * CZ]) * (DH**-0.5)
            qp[i, h * level : (h + 1) * level, :] = key_side.astype(bf16)

    top, denom, mixed = [None, None], [None, None], [None, None]
    for ks in turns:
        for k in ks:
            for copy in landing.get(k, ()):
                copy.wait_recv()
            for copy in onward.get(k, ()):
                copy.start()
        ats = [pl.ds(pl.multiple_of(lax.rem(z + nz - k, nz) * level, level), level) for k in ks]
        offsets = jnp.concatenate([bias_f[:, at] for at in ats], axis=1)
        for i in range(2):
            rows = jnp.concatenate([nb[i, at, :] for at in ats], axis=0)
            scores = dot_t(qp[i], rows) + offsets
            peak = jnp.max(scores, axis=1, keepdims=True)
            if ks == (0,):
                weights = jnp.exp(scores - peak)
                denom[i] = jnp.sum(weights, axis=1, keepdims=True)
                mixed[i] = dot(weights.astype(bf16), rows)
            else:
                peak = jnp.maximum(peak, top[i])
                shrink = jnp.exp(top[i] - peak)
                weights = jnp.exp(scores - peak)
                denom[i] = denom[i] * shrink + jnp.sum(weights, axis=1, keepdims=True)
                mixed[i] = mixed[i] * shrink + dot(weights.astype(bf16), rows)
            top[i] = peak

    for i in range(2):
        values = dot((mixed[i] / denom[i]).astype(bf16), wqkvg[:, 2 * CZ : 3 * CZ])
        attended = jnp.zeros((level, CZ), f32)
        for h in range(H):
            attended = jnp.where(head_lane == h, values[h * level : (h + 1) * level, :], attended)
        ub[i] = dot((gates[i] * attended).astype(bf16), wout[...]).astype(bf16)

    def upd_copy(q, src_p):
        return remote(
            ub.at[:, pl.ds(q * tok, tok), :],
            upd_in.at[src_p],
            up_s.at[q],
            up_r.at[src_p],
            d,
            z * 4 + q,
        )

    for q in others:
        upd_copy(q, p).start()
    upd_in[p] = ub[:, pl.ds(pl.multiple_of(p * tok, tok), tok), :]
    for q in others:
        pair_copy(q, q).wait_recv()
    for q in range(4):
        for i in range(2):
            pair_ref[2 * q + i] = pair_in[q, i]
    for q in others:
        upd_copy(q, q).wait_recv()
    for q in range(4):
        for i in range(2):
            upd_ref[2 * q + i] = upd_in[q, i]

    tb_own_x.wait_send()
    tb_own_c.wait_send()
    tb_x_c.wait_send()
    drain_band()
    band_c(c).wait_send()
    for i in range(gh):
        for q in range(4):

            @pl.when(jnp.logical_not(jnp.logical_and(x * gh + i == d, q == p)))
            def _():
                reduce_copy(i, q, x * gh + i, d, c).wait_send()

    for copy in first + [copy for copies in onward.values() for copy in copies]:
        copy.wait_send()
    for q in others:
        pair_copy(q, p).wait_send()
        upd_copy(q, p).wait_send()


def body(
    nd,
    nr,
    alignment_left,
    alignment_right,
    window_starts,
    outer_product_weight,
    outer_product_bias,
    query_key_value_gate_weight,
    output_weight,
    triangle_pair_bias,
    residue_chain,
    interchain_offset,
):
    seqs, cols = alignment_left.shape
    tok = cols // CH
    nz = nr // 4
    chunk = seqs // nz
    quarter = nd // 4 * U * CH
    keys = nr * tok
    anywhere = pl.BlockSpec(memory_space=pl.ANY)
    vmem = pl.BlockSpec(memory_space=pltpu.VMEM)
    smem = pl.BlockSpec(memory_space=pltpu.SMEM)
    sem = pltpu.SemaphoreType.DMA
    out = jax.ShapeDtypeStruct((U, tok, CZ), bf16)
    return pl.pallas_call(
        functools.partial(kernel, nd, nr),
        out_shape=(out, out),
        in_specs=[smem, smem] + [anywhere] * 8,
        out_specs=(vmem, vmem),
        scratch_shapes=[
            pltpu.VMEM((2, seqs, cols), bf16),
            pltpu.VMEM((CH * CH, CZ), bf16),
            pltpu.VMEM((1, CZ), f32),
            pltpu.VMEM((CZ, 4 * CZ), bf16),
            pltpu.VMEM((CZ, CZ), bf16),
            pltpu.VMEM((1, keys), jnp.int32),
            pltpu.VMEM((4, H, tok, keys), bf16),
            pltpu.VMEM((nz, chunk, cols), bf16),
            pltpu.VMEM((nz * cols // 128, chunk, 128), bf16),
            pltpu.VMEM((4, chunk, quarter), bf16),
            pltpu.VMEM((4, chunk, quarter), bf16),
            pltpu.VMEM((2, seqs, quarter), bf16),
            pltpu.VMEM((seqs // 128, cols, 128), f32),
            pltpu.VMEM((2 * cols, seqs), bf16),
            pltpu.VMEM((CH * CH, CZ), f32),
            pltpu.VMEM((CH * 128, 4 * CZ), bf16),
            pltpu.VMEM((H * 4 * tok, keys), f32),
            pltpu.VMEM((nd // 4 * 2 * 2 * tok, CH * 128), bf16),
            pltpu.VMEM((nd // 2, 4, 2, 2, tok, CZ), bf16),
            pltpu.VMEM((2 * nd, 2, 2, tok, CZ), bf16),
            pltpu.VMEM((4, 2, tok, CZ), bf16),
            pltpu.VMEM((4, 2, tok, CZ), bf16),
            pltpu.VMEM((2, keys, CZ), bf16),
            pltpu.VMEM((2, H * 4 * tok, CZ), bf16),
            pltpu.VMEM((2, 4 * tok, CZ), bf16),
            pltpu.VMEM((4, 2, tok, CZ), bf16),
            sem((8,)),
            sem((nz,)),
            sem((nz,)),
            sem((3,)),
            sem((3,)),
            sem((4,)),
            sem((4,)),
            sem((nz,)),
            sem((nz,)),
            sem((1,)),
            sem((1,)),
            sem((1,)),
            sem((1,)),
            sem((2 * nd,)),
            sem((2 * nd,)),
            sem((4,)),
            sem((4,)),
            sem((nz,)),
            sem((nz,)),
            sem((4,)),
            sem((4,)),
        ],
        compiler_params=pltpu.CompilerParams(
            collective_id=0, has_side_effects=True, vmem_limit_bytes=VMEM_BYTES
        ),
        cost_estimate=pl.CostEstimate(
            flops=4_000_000_000, bytes_accessed=4_000_000, transcendentals=1_100_000
        ),
    )(
        window_starts,
        interchain_offset,
        alignment_left,
        alignment_right,
        outer_product_weight,
        outer_product_bias.reshape(1, CZ),
        query_key_value_gate_weight,
        output_weight,
        triangle_pair_bias,
        residue_chain.reshape(1, keys),
    )


def solution(mesh):
    in_specs = (
        P("depth", "res"),
        P("depth", "res"),
        P(),
        P(),
        P(),
        P(),
        P(),
        P(None, "res", None),
        P(),
        P(),
    )
    out_specs = (P("depth", "res", None), P("depth", "res", None))
    return jax.shard_map(
        functools.partial(body, mesh.shape["depth"], mesh.shape["res"]),
        mesh=mesh,
        in_specs=in_specs,
        out_specs=out_specs,
        check_vma=False,
    )
```

```python
import functools

import jax
import jax.numpy as jnp
from jax import lax
from jax.experimental import pallas as pl
from jax.experimental.pallas import tpu as pltpu
from jax.sharding import PartitionSpec as P

CH = 32
CZ = 128
H = 4
DH = 32
U = 8
EPS = 1e-05
VMEM_BYTES = 63 * 1024 * 1024
MESH = pl.DeviceIdType.MESH
f32 = jnp.float32
bf16 = jnp.bfloat16


def dot(a, b):
    return jnp.dot(a, b, preferred_element_type=f32)


def dot_t(a, b):
    return lax.dot_general(a, b, (((1,), (1,)), ((), ())), preferred_element_type=f32)


def kernel(
    nd,
    nr,
    ws_ref,
    off_ref,
    left_hbm,
    right_hbm,
    w_hbm,
    ob_hbm,
    wqkvg_hbm,
    wout_hbm,
    tb_hbm,
    chain_hbm,
    pair_ref,
    upd_ref,
    right,
    w,
    ob,
    wqkvg,
    wout,
    chain_v,
    tb,
    l1,
    l1_tiles,
    picks,
    picks_in,
    band,
    r_t,
    r_p,
    w_f,
    wbd,
    bias_f,
    xs,
    part,
    rs_in,
    pair_out,
    pair_in,
    nb,
    qp,
    ub,
    upd_in,
    in_sem,
    s0_s,
    s0_r,
    tb_s,
    tb_r,
    pk_s,
    pk_r,
    bz_s,
    bz_r,
    rx_s,
    rx_r,
    bc_s,
    bc_r,
    rs_s,
    rs_r,
    pr_s,
    pr_r,
    nz_s,
    nz_r,
    up_s,
    up_r,
):
    seqs, cols = left_hbm.shape
    tok = cols // CH
    nz = nr // 4
    chunk = seqs // nz
    groups = nd
    gq = groups // 4
    gh = groups // 2
    tiles_dev = cols // 128
    keys = nr * tok
    level = 4 * tok

    d = lax.axis_index("depth")
    r = lax.axis_index("res")
    z = r // 4
    p = r % 4
    x = p // 2
    c = p % 2
    p_x = (1 - x) * 2 + c
    p_c = x * 2 + (1 - c)
    p_xc = (1 - x) * 2 + (1 - c)

    def remote(src, dst, send, recv, depth, res):
        return pltpu.make_async_remote_copy(
            src_ref=src,
            dst_ref=dst,
            send_sem=send,
            recv_sem=recv,
            device_id=(depth, res),
            device_id_type=MESH,
        )

    barrier = pltpu.get_barrier_semaphore()
    others = (p_x, p_c, p_xc)
    for k in range(1, nz):
        pl.semaphore_signal(
            barrier, inc=1, device_id=(d, lax.rem(z + k, nz) * 4 + p), device_id_type=MESH
        )
    for q in others:
        pl.semaphore_signal(barrier, inc=1, device_id=(d, z * 4 + q), device_id_type=MESH)
    for k in range(1, nd):
        for e in range(2):
            pl.semaphore_signal(
                barrier,
                inc=1,
                device_id=(lax.rem(d + k, nd), z * 4 + d // gh * 2 + e),
                device_id_type=MESH,
            )

    inputs = [
        pltpu.make_async_copy(src, dst, in_sem.at[i])
        for i, (src, dst) in enumerate(
            (
                (right_hbm, right.at[x]),
                (w_hbm, w),
                (ob_hbm, ob),
                (wqkvg_hbm, wqkvg),
                (wout_hbm, wout),
                (chain_hbm, chain_v),
                (tb_hbm, tb.at[p]),
                (left_hbm.at[pl.ds(z * chunk, chunk), :], l1.at[z]),
            )
        )
    ]
    for copy in inputs:
        copy.start()
    apart = (d // gh - x) * (d // gh - x)
    pl.semaphore_wait(barrier, nz - 1 + 3 + 4 * (gh - 1) + 4 * apart)

    def scatter_copy(k):
        zz = lax.rem(z + k, nz)
        return remote(
            left_hbm.at[pl.ds(zz * chunk, chunk), :],
            l1.at[z],
            s0_s.at[k],
            s0_r.at[k],
            d,
            zz * 4 + p,
        )

    order = sorted(range(1, nz), key=lambda k: -min(k, nz - k))
    for k in order:
        scatter_copy(k).start()

    right_copy = remote(right_hbm, right.at[x], rx_s.at[0], rx_r.at[0], d, z * 4 + p_x)
    right_copy.start()

    for copy in inputs:
        copy.wait()
    tb_own_x = remote(tb.at[p], tb.at[p], tb_s.at[0], tb_r.at[0], d, z * 4 + p_x)
    tb_own_c = remote(tb.at[p], tb.at[p], tb_s.at[1], tb_r.at[1], d, z * 4 + p_c)
    tb_x_c = remote(tb.at[p_x], tb.at[p_x], tb_s.at[2], tb_r.at[2], d, z * 4 + p_c)

    def turn_right(b):
        for q in range(seqs // 128):
            r_t[q] = jnp.transpose(right[b, q * 128 : (q + 1) * 128, :].astype(f32))
        for i in range(CH):
            row = pl.ds(pl.multiple_of((2 * i + b) * tok, tok), tok)
            for q in range(seqs // 128):
                r_p[row, q * 128 : (q + 1) * 128] = r_t[q, pl.ds(i, tok, stride=CH), :].astype(bf16)

    turn_right(x)
    w_f[...] = w[...].astype(f32)
    wbd[...] = jnp.zeros_like(wbd)
    for i in range(CH):
        w_i = w_f[pl.ds(i, CH, stride=CH), :].astype(bf16)
        for b in range(4):
            wbd[i * 128 + b * CH : i * 128 + (b + 1) * CH, b * CZ : (b + 1) * CZ] = w_i

    for k in order:
        scatter_copy(k).wait()

    for i in range(nz):
        for t in range(tiles_dev):
            l1_tiles[i * tiles_dev + t] = l1[i, :, t * 128 : (t + 1) * 128]

    last_tile = nr * tiles_dev - 1
    for g in range(groups):
        start = ws_ref[g]
        first = lax.div(start, 4)
        shift = start - 4 * first
        pieces = []
        for t in range(3):
            tile = jnp.minimum(first + t, last_tile)
            src = lax.div(tile, tiles_dev)
            zz = lax.div(src, 4)
            piece = l1_tiles[zz * tiles_dev + tile - src * tiles_dev].astype(f32)
            pieces.append(jnp.where(src - 4 * zz == p, piece, 0.0))
        wide = jnp.concatenate(pieces, axis=1)
        picked = wide[:, :256]
        for b in range(1, 4):
            picked = jnp.where(shift == b, wide[:, b * CH : b * CH + 256], picked)
        picks[g // gq, :, (g % gq) * 256 : (g % gq + 1) * 256] = picked.astype(bf16)

    picks_out = [
        remote(picks.at[q], picks_in.at[p], pk_s.at[q], pk_r.at[p], d, z * 4 + q) for q in others
    ]
    for copy in picks_out:
        copy.start()
    for q, copy in zip(others, picks_out):
        copy.wait_send()
        remote(picks.at[q], picks_in.at[q], pk_s.at[q], pk_r.at[q], d, z * 4 + q).wait_recv()
    picks_in[p] = picks[p]
    merged = picks_in[0].astype(f32)
    for q in range(1, 4):
        merged = merged + picks_in[q].astype(f32)
    band[c, pl.ds(pl.multiple_of(z * chunk, chunk), chunk), :] = merged.astype(bf16)

    near = sorted(range(1, nz), key=lambda k: min(k, nz - k))

    def gather(block, send, recv):
        def copy(k, back):
            zz = lax.rem(z + (nz - k if back else k), nz)
            ref = block(zz if back else z)
            return remote(ref, ref, send.at[k], recv.at[k], d, zz * 4 + p)

        for k in near:
            copy(k, False).start()

        def arrive(k):
            copy(k, True).wait_recv()

        def drain():
            for k in near:
                copy(k, False).wait_send()

        return arrive, drain

    band_arrive, drain_band = gather(
        lambda zz: band.at[c, pl.ds(zz * chunk, chunk), :], bz_s, bz_r
    )

    def bias_of(q):
        chain_f = chain_v[...].astype(f32)
        key_at = lax.broadcasted_iota(jnp.int32, (tok, keys), 1)
        query_at = lax.broadcasted_iota(jnp.int32, (tok, keys), 0) + (z * level + q * tok)
        own = jnp.sum(jnp.where(key_at == query_at, chain_f, 0.0), axis=1, keepdims=True)
        differ = (own != chain_f).astype(f32)
        for h in range(H):
            at = pl.ds(pl.multiple_of(h * level + q * tok, tok), tok)
            bias_f[at, :] = tb[q, h].astype(f32) + off_ref[h] * differ

    tb_own_c.start()
    right_copy.wait()
    tb_own_x.start()
    turn_right(1 - x)
    bias_of(p)
    tb_own_c.wait_recv()
    bias_of(p_c)
    for k in near:
        band_arrive(k)

    def band_c(q):
        return remote(band.at[q], band.at[q], bc_s.at[0], bc_r.at[0], d, z * 4 + p_c)

    band_c(c).start()

    def reduce_copy(i, q, g, depth, e):
        return remote(
            part.at[i, q], rs_in.at[depth * 2 + e], rs_s.at[i * 4 + q], rs_r.at[depth * 2 + e], g, z * 4 + q
        )

    def outer(e):
        for i in range(gq):
            y = dot(r_p[...], band[e, :, i * 256 : (i + 1) * 256]).astype(bf16)
            for t in range(2):
                row = (2 * i + t) * 2 * tok
                for b in range(CH):
                    xs[row : row + 2 * tok, b * 128 : (b + 1) * 128] = y[
                        b * 2 * tok : (b + 1) * 2 * tok, t * 128 : (t + 1) * 128
                    ]
        out = dot(xs[...], wbd[...]).astype(bf16)
        for i in range(gq):
            at = e * gq + i
            g = x * gh + at
            for q in range(4):
                for n in range(2):
                    u = 2 * q + n
                    for b in range(2):
                        row = ((2 * i + u // 4) * 2 + b) * tok
                        part[at, q, n, b] = out[row : row + tok, (u % 4) * CZ : (u % 4 + 1) * CZ]

                here = jnp.logical_and(g == d, q == p)

                @pl.when(jnp.logical_not(here))
                def _():
                    reduce_copy(at, q, g, d, c).start()

                @pl.when(here)
                def _():
                    rs_in[d * 2 + c] = part[at, q]

    outer(c)
    band_c(1 - c).wait_recv()
    outer(1 - c)
    tb_own_x.wait_recv()
    tb_x_c.start()
    bias_of(p_x)
    tb_x_c.wait_recv()
    bias_of(p_xc)

    def reduced(depth, e):
        return remote(
            part.at[0, 0],
            rs_in.at[depth * 2 + e],
            rs_s.at[0],
            rs_r.at[depth * 2 + e],
            depth,
            z * 4 + d // gh * 2 + e,
        )

    for e in range(2):
        for k in range(nd):
            source = lax.rem(d + k, nd)
            if k == 0:

                @pl.when(jnp.logical_not(jnp.logical_and(d // gh == x, c == e)))
                def _():
                    reduced(d, e).wait_recv()

            else:
                reduced(source, e).wait_recv()

        total = rs_in[e].astype(f32)
        for k in range(1, nd):
            total = total + rs_in[2 * k + e].astype(f32)
        total = total.reshape(4 * tok, CZ)
        pair = (total * (1.0 / (seqs * nd)) + ob[...]).astype(bf16)
        value = pair.astype(f32)
        centred = value - jnp.mean(value, axis=1, keepdims=True)
        variance = jnp.mean(centred * centred, axis=1, keepdims=True)
        normed = (centred * lax.rsqrt(variance + EPS)).astype(bf16)
        for n in range(2):
            for b in range(2):
                piece = slice((2 * n + b) * tok, (2 * n + b + 1) * tok)
                to = pl.ds(pl.multiple_of((z * 4 + 2 * b + e) * tok, tok), tok)
                nb[n, to, :] = normed[piece]
                pair_out[2 * b + e, n] = pair[piece]

    def rows_copy(k, to, at, i):
        ref = nb.at[i, pl.ds(lax.rem(z + nz + at, nz) * level, level), :]
        n = k * 2 + i
        return remote(ref, ref, nz_s.at[n], nz_r.at[n], d, lax.rem(z + nz + to, nz) * 4 + p)

    if nz == 8:
        first = [rows_copy(k, k, 0, i) for ks in ((2, 6), (1, 7)) for i in range(2) for k in ks]
        onward = {
            (2, 0): [rows_copy(3, 1, -2, 0), rows_copy(4, 2, -2, 0)],
            (2, 1): [rows_copy(3, 1, -2, 1)],
            (6, 0): [rows_copy(5, -1, 2, 0)],
            (6, 1): [rows_copy(5, -1, 2, 1), rows_copy(4, -2, 2, 1)],
        }
        turns = [(0,), (2, 6), (1, 7), (3, 5), (4,)]
    else:
        first = [rows_copy(k, k, 0, i) for k in near for i in range(2)]
        onward = {}
        turns = [(0,)] + [(k, nz - k) for k in range(1, nz // 2)] + [(nz // 2,)]
    for copy in first:
        copy.start()

    def pair_copy(q, src_p):
        return remote(
            pair_out.at[q], pair_in.at[src_p], pr_s.at[q], pr_r.at[src_p], d, z * 4 + q
        )

    for q in others:
        pair_copy(q, p).start()
    pair_in[p] = pair_out[p]

    head_lane = lax.broadcasted_iota(jnp.int32, (level, CZ), 1) // DH
    gates = []
    for i in range(2):
        here = nb[i, pl.ds(pl.multiple_of(z * level, level), level), :]
        queries = dot(here, wqkvg[:, :CZ]).astype(bf16)
        gates.append(jax.nn.sigmoid(dot(here, wqkvg[:, 3 * CZ :]).astype(bf16).astype(f32)))
        for h in range(H):
            own_head = jnp.where(head_lane == h, queries, jnp.zeros_like(queries))
            key_side = dot_t(own_head, wqkvg[:, CZ : 2 * CZ]) * (DH**-0.5)
            qp[i, h * level : (h + 1) * level, :] = key_side.astype(bf16)

    top, denom, mixed = [None, None], [None, None], [None, None]
    for ks in turns:
        if ks != (0,):
            for i in range(2):
                for k in ks:
                    rows_copy(k, 0, -k, i).wait_recv()
                    for copy in onward.get((k, i), ()):
                        copy.start()
        ats = [pl.ds(pl.multiple_of(lax.rem(z + nz - k, nz) * level, level), level) for k in ks]
        offsets = jnp.concatenate([bias_f[:, at] for at in ats], axis=1)
        for i in range(2):
            rows = jnp.concatenate([nb[i, at, :] for at in ats], axis=0)
            scores = dot_t(qp[i], rows) + offsets
            peak = jnp.max(scores, axis=1, keepdims=True)
            if ks == (0,):
                weights = jnp.exp(scores - peak)
                denom[i] = jnp.sum(weights, axis=1, keepdims=True)
                mixed[i] = dot(weights.astype(bf16), rows)
            else:
                peak = jnp.maximum(peak, top[i])
                shrink = jnp.exp(top[i] - peak)
                weights = jnp.exp(scores - peak)
                denom[i] = denom[i] * shrink + jnp.sum(weights, axis=1, keepdims=True)
                mixed[i] = mixed[i] * shrink + dot(weights.astype(bf16), rows)
            top[i] = peak

    for i in range(2):
        values = dot((mixed[i] / denom[i]).astype(bf16), wqkvg[:, 2 * CZ : 3 * CZ])
        attended = jnp.zeros((level, CZ), f32)
        for h in range(H):
            attended = jnp.where(head_lane == h, values[h * level : (h + 1) * level, :], attended)
        ub[i] = dot((gates[i] * attended).astype(bf16), wout[...]).astype(bf16)

    def upd_copy(q, src_p):
        return remote(
            ub.at[:, pl.ds(q * tok, tok), :],
            upd_in.at[src_p],
            up_s.at[q],
            up_r.at[src_p],
            d,
            z * 4 + q,
        )

    for q in others:
        upd_copy(q, p).start()
    upd_in[p] = ub[:, pl.ds(pl.multiple_of(p * tok, tok), tok), :]
    for q in others:
        pair_copy(q, q).wait_recv()
    for q in range(4):
        for i in range(2):
            pair_ref[2 * q + i] = pair_in[q, i]
    for q in others:
        upd_copy(q, q).wait_recv()
    for q in range(4):
        for i in range(2):
            upd_ref[2 * q + i] = upd_in[q, i]

    tb_own_x.wait_send()
    tb_own_c.wait_send()
    tb_x_c.wait_send()
    drain_band()
    band_c(c).wait_send()
    for i in range(gh):
        for q in range(4):

            @pl.when(jnp.logical_not(jnp.logical_and(x * gh + i == d, q == p)))
            def _():
                reduce_copy(i, q, x * gh + i, d, c).wait_send()

    for copy in first + [copy for copies in onward.values() for copy in copies]:
        copy.wait_send()
    for q in others:
        pair_copy(q, p).wait_send()
        upd_copy(q, p).wait_send()


def body(
    nd,
    nr,
    alignment_left,
    alignment_right,
    window_starts,
    outer_product_weight,
    outer_product_bias,
    query_key_value_gate_weight,
    output_weight,
    triangle_pair_bias,
    residue_chain,
    interchain_offset,
):
    seqs, cols = alignment_left.shape
    tok = cols // CH
    nz = nr // 4
    chunk = seqs // nz
    quarter = nd // 4 * U * CH
    keys = nr * tok
    anywhere = pl.BlockSpec(memory_space=pl.ANY)
    vmem = pl.BlockSpec(memory_space=pltpu.VMEM)
    smem = pl.BlockSpec(memory_space=pltpu.SMEM)
    sem = pltpu.SemaphoreType.DMA
    out = jax.ShapeDtypeStruct((U, tok, CZ), bf16)
    return pl.pallas_call(
        functools.partial(kernel, nd, nr),
        out_shape=(out, out),
        in_specs=[smem, smem] + [anywhere] * 8,
        out_specs=(vmem, vmem),
        scratch_shapes=[
            pltpu.VMEM((2, seqs, cols), bf16),
            pltpu.VMEM((CH * CH, CZ), bf16),
            pltpu.VMEM((1, CZ), f32),
            pltpu.VMEM((CZ, 4 * CZ), bf16),
            pltpu.VMEM((CZ, CZ), bf16),
            pltpu.VMEM((1, keys), jnp.int32),
            pltpu.VMEM((4, H, tok, keys), bf16),
            pltpu.VMEM((nz, chunk, cols), bf16),
            pltpu.VMEM((nz * cols // 128, chunk, 128), bf16),
            pltpu.VMEM((4, chunk, quarter), bf16),
            pltpu.VMEM((4, chunk, quarter), bf16),
            pltpu.VMEM((2, seqs, quarter), bf16),
            pltpu.VMEM((seqs // 128, cols, 128), f32),
            pltpu.VMEM((2 * cols, seqs), bf16),
            pltpu.VMEM((CH * CH, CZ), f32),
            pltpu.VMEM((CH * 128, 4 * CZ), bf16),
            pltpu.VMEM((H * 4 * tok, keys), f32),
            pltpu.VMEM((nd // 4 * 2 * 2 * tok, CH * 128), bf16),
            pltpu.VMEM((nd // 2, 4, 2, 2, tok, CZ), bf16),
            pltpu.VMEM((2 * nd, 2, 2, tok, CZ), bf16),
            pltpu.VMEM((4, 2, tok, CZ), bf16),
            pltpu.VMEM((4, 2, tok, CZ), bf16),
            pltpu.VMEM((2, keys, CZ), bf16),
            pltpu.VMEM((2, H * 4 * tok, CZ), bf16),
            pltpu.VMEM((2, 4 * tok, CZ), bf16),
            pltpu.VMEM((4, 2, tok, CZ), bf16),
            sem((8,)),
            sem((nz,)),
            sem((nz,)),
            sem((3,)),
            sem((3,)),
            sem((4,)),
            sem((4,)),
            sem((nz,)),
            sem((nz,)),
            sem((1,)),
            sem((1,)),
            sem((1,)),
            sem((1,)),
            sem((2 * nd,)),
            sem((2 * nd,)),
            sem((4,)),
            sem((4,)),
            sem((2 * nz,)),
            sem((2 * nz,)),
            sem((4,)),
            sem((4,)),
        ],
        compiler_params=pltpu.CompilerParams(
            collective_id=0, has_side_effects=True, vmem_limit_bytes=VMEM_BYTES
        ),
        cost_estimate=pl.CostEstimate(
            flops=4_000_000_000, bytes_accessed=4_000_000, transcendentals=1_100_000
        ),
    )(
        window_starts,
        interchain_offset,
        alignment_left,
        alignment_right,
        outer_product_weight,
        outer_product_bias.reshape(1, CZ),
        query_key_value_gate_weight,
        output_weight,
        triangle_pair_bias,
        residue_chain.reshape(1, keys),
    )


def solution(mesh):
    in_specs = (
        P("depth", "res"),
        P("depth", "res"),
        P(),
        P(),
        P(),
        P(),
        P(),
        P(None, "res", None),
        P(),
        P(),
    )
    out_specs = (P("depth", "res", None), P("depth", "res", None))
    return jax.shard_map(
        functools.partial(body, mesh.shape["depth"], mesh.shape["res"]),
        mesh=mesh,
        in_specs=in_specs,
        out_specs=out_specs,
        check_vma=False,
    )
```
